32 devices in a mesh: pp: 4 (over y, x), ep: 8 (over z, core).
Axes of the slice: x: 2, y: 2, z: 4, core: 2. Of those that a mesh axis runs over, the one named last changes fastest.
Arguments:
- prev_out: bfloat16 [4, 1024, 7168], P('pp', 'ep'), may hold values from -6 to 6
- fwd_experts: int32 [4, 1024, 2], P('pp', 'ep'), may hold values from 0 to 3, all different within a row; in each aligned block of 128 rows (0 to 127, 128 to 255, ..., all dimensions but the last counted through in order) at most 96 rows name the same one
- expert_weights: bfloat16 [4, 8, 7168, 1024], P('pp', 'ep'), may hold values from -0.0625 to 0.0625
- bwd_experts: int32 [4, 1024, 2], P('pp', 'ep'), may hold values from 0 to 3, all different within a row; in each aligned block of 128 rows (0 to 127, 128 to 255, ..., all dimensions but the last counted through in order) at most 96 rows name the same one
- grad_hidden: bfloat16 [4, 8, 8, 96, 512], P('pp', 'ep'), may hold values from -6 to 6
- saved_pre: bfloat16 [4, 8, 8, 96, 1024], P('pp', 'ep'), may hold values from -6 to 6
Outputs:
- hidden_out: bfloat16 [4, 8, 8, 96, 512], P('pp', 'ep')
- grad_rows: bfloat16 [4, 1024, 7168], P('pp', 'ep')
The draws below stay inside these ranges and needn't reach their ends.
Inputs may be any that keep to these rules, and one draw needn't show every extreme that they name: `fwd_experts`: each row names 2 different experts, and within the 128 rows of one device no expert is named more than 96 times. `bwd_experts`: each row names 2 different experts, and within the 128 rows of one device no expert is named more than 96 times.
All inputs are finite; a program needn't handle non-finite values.
Results may differ from the reference program's by a relative error of at most 0.0066.
Values may be sent and summed in bfloat16 or wider, within the bound.
A program may use at most 128 MiB of HBM per device.

```python
import math
from functools import partial
import jax
import jax.numpy as jnp
import numpy as np
from jax import lax

D = 7168
HID_DEV = 512
TOP = 2
SECTIONS = 4
EXPERTS = 4
TOK_DEV = 128
TOKENS = 1024
CAP = 96
N_EP = 8


def steps_of(rng, shape, split, least, high):
    gain = 1.0
    for axis_at, blocks in split:
        draws = jax.random.uniform(jax.random.fold_in(jax.random.fold_in(rng, 6), axis_at), (blocks,), jnp.float32, least / len(split), high / len(split))
        gain = gain * jnp.repeat(jnp.exp(draws), shape[axis_at] // blocks).reshape((-1,) + (1,) * (len(shape) - 1 - axis_at))
    return gain


def shared_out(own_key, own, number, rows, number_of, top, limit, lean):
    sequence = jax.random.permutation(own_key, number_of)
    packed, common = load_shares(number_of, rows * top, limit, lean, True), load_shares(number_of, rows * top, limit, lean, False)
    places = jnp.arange(number_of)

    def named(lengths, offset_by):
        used = int((lengths > 0).sum())
        fixed = max(1, used // 4)
        passed = fixed + (places - fixed + offset_by * (used - fixed)) % max(1, number_of - fixed)
        return jnp.zeros((number_of,), jnp.int32).at[sequence[jnp.where(places < fixed, places, passed)]].set(jnp.asarray(lengths, jnp.int32))

    lengths = jnp.where(number % 4 == 0, named(packed, number // 4), named(common, number - number // 4 - 1))
    mixed = jax.random.permutation(jax.random.fold_in(own, 3), number_of)
    donor, sink = mixed[0:number_of // 2 * 2:2], mixed[1:number_of // 2 * 2:2]
    room = jnp.minimum(lengths[donor] - 1, limit - lengths[sink]) // 2
    room = jnp.where((donor == sequence[0]) | (sink == sequence[0]) | (lengths[sink] == 0), 0, jnp.maximum(room, 0))
    passed = jax.random.randint(jax.random.fold_in(own, 4), (number_of // 2,), 0, 1 << 20) % (room + 1)
    lengths = lengths.at[donor].add(-passed).at[sink].add(passed)
    items = jnp.searchsorted(jnp.cumsum(lengths), jnp.arange(rows * top), side="right").astype(jnp.int32)
    grid = items.reshape(top, rows).T
    grid = grid[jax.random.permutation(jax.random.fold_in(own, 1), rows)]
    offset_by = jax.random.randint(jax.random.fold_in(own, 2), (rows, 1), 0, top)
    return jnp.take_along_axis(grid, (jnp.arange(top)[None, :] + offset_by) % top, axis=1)


def load_shares(count, total, bound, slope, full):
    weights = [(1 << 20) // math.isqrt(grade ** slope) + 1 for grade in range(1, count + 1)]
    largest = bound if full else min(bound, max(-(-total // count), total * weights[0] // sum(weights)))
    least = 1 if total - largest >= count - 1 else 0
    holding, surplus = [largest] + [least] * (count - 1), total - largest - least * (count - 1)
    while surplus > 0:
        candidates = [i for i in range(1, count) if holding[i] < largest] or [i for i in range(1, count) if holding[i] < bound]
        mass, budget = sum([weights[i] for i in candidates]), surplus
        for i in candidates:
            more = min(bound - holding[i], max(1, budget * weights[i] // mass), surplus)
            holding[i] = holding[i] + more
            surplus = surplus - more
    return np.array(holding)


def centred(own_key, extent, scale, limit, split=(), held_as=jnp.bfloat16):
    array = scale * jax.random.normal(own_key, extent, jnp.float32)
    if split:
        array = array * steps_of(own_key, extent, split, -0.22, 0.18)
    return jnp.clip(array, -limit, limit).astype(held_as)


def setup_inputs(seed: int = 0) -> dict:
    seeds = jax.random.split(jax.random.key(seed), 7)
    prev_out = centred(seeds[0], (SECTIONS, TOKENS, D), 1.0, 6.0, ((0, 4), (1, 8)))
    fwd_experts_keys = jax.random.split(jax.random.fold_in(seeds[1], 1), SECTIONS * TOKENS // TOK_DEV)
    fwd_experts_turns = jax.random.permutation(jax.random.fold_in(seeds[1], 3), SECTIONS * TOKENS // TOK_DEV)
    fwd_experts = jax.vmap(lambda own, number: shared_out(jax.random.fold_in(seeds[1], 2), own, number, TOK_DEV, EXPERTS, TOP, CAP, 2))(fwd_experts_keys, fwd_experts_turns).reshape((SECTIONS, TOKENS, TOP))
    expert_weights = centred(seeds[2], (SECTIONS, N_EP, D, 2 * HID_DEV), D ** -0.5, 0.0625, ((0, 4), (1, 8)))
    bwd_experts_keys = jax.random.split(jax.random.fold_in(seeds[3], 1), SECTIONS * TOKENS // TOK_DEV)
    bwd_experts_turns = jax.random.permutation(jax.random.fold_in(seeds[3], 3), SECTIONS * TOKENS // TOK_DEV)
    bwd_experts = jax.vmap(lambda own, number: shared_out(jax.random.fold_in(seeds[3], 2), own, number, TOK_DEV, EXPERTS, TOP, CAP, 2))(bwd_experts_keys, bwd_experts_turns).reshape((SECTIONS, TOKENS, TOP))
    grad_hidden = centred(seeds[4], (SECTIONS, N_EP, N_EP, CAP, HID_DEV), 1.0, 6.0, ((0, 4), (1, 8)))
    saved_pre = centred(seeds[5], (SECTIONS, N_EP, N_EP, CAP, 2 * HID_DEV), 1.0, 6.0, ((0, 4), (1, 8)))
    return dict(prev_out=prev_out, fwd_experts=fwd_experts, expert_weights=expert_weights, bwd_experts=bwd_experts, grad_hidden=grad_hidden, saved_pre=saved_pre)


def slot_table(route_ids, expert_count, capacity):
    token_count, choice_count = route_ids.shape
    flattened = route_ids.reshape(token_count * choice_count)
    onehot = (flattened[:, None] == jnp.arange(expert_count, dtype=jnp.int32)[None, :]).astype(jnp.int32)
    earlier = jnp.cumsum(onehot, axis=0) - onehot
    slot_index = jnp.sum(earlier * onehot, axis=1)
    slot_match = (slot_index[:, None] == jnp.arange(capacity, dtype=jnp.int32)[None, :]).astype(jnp.float32)
    expert_match = onehot.astype(jnp.float32)
    joined = jnp.einsum('re,rc->rec', expert_match, slot_match).reshape(token_count, choice_count, expert_count, capacity)
    return jnp.transpose(jnp.sum(joined, axis=1), (1, 2, 0))


def swiglu_forward(received, weights):
    hid_units = weights.shape[1] // 2
    projected = jnp.einsum('scd,dh->sch', received.astype(jnp.float32), weights.astype(jnp.float32))
    return (jax.nn.silu(projected[..., :hid_units]) * projected[..., hid_units:]).astype(jnp.bfloat16)


def swiglu_backward(upstream, saved):
    hid_units = upstream.shape[-1]
    pre_float = saved.astype(jnp.float32)
    gate_pre = pre_float[..., :hid_units]
    up_pre = pre_float[..., hid_units:]
    sigmoid_gate = jax.nn.sigmoid(gate_pre)
    upstream_float = upstream.astype(jnp.float32)
    grad_gate = upstream_float * up_pre * sigmoid_gate * (1.0 + gate_pre * (1.0 - sigmoid_gate))
    grad_up = upstream_float * gate_pre * sigmoid_gate
    return jnp.concatenate([grad_gate, grad_up], axis=-1).astype(jnp.bfloat16)


def reference(prev_out, fwd_experts, expert_weights, bwd_experts, grad_hidden, saved_pre):
    make_tables = jax.vmap(partial(slot_table, expert_count=EXPERTS, capacity=CAP))
    rows_in = jnp.roll(prev_out, 1, axis=0)

    def section_forward(section_args):
        section_rows, route_ids, weights = section_args
        blocks = section_rows.reshape(N_EP, TOK_DEV, D).astype(jnp.float32)
        tables = make_tables(route_ids.reshape(N_EP, TOK_DEV, TOP))
        picked = lax.optimization_barrier(jnp.einsum('sect,std->secd', tables, blocks).astype(jnp.bfloat16))

        def one_shard(shard_index):
            received = jnp.take(picked, shard_index // 2, axis=1)
            return swiglu_forward(received, jnp.take(weights, shard_index, axis=0))

        return lax.map(one_shard, jnp.arange(N_EP, dtype=jnp.int32))

    hidden_out = lax.map(section_forward, (rows_in, fwd_experts, expert_weights))

    def section_backward(section_args):
        route_ids, weights, upstream, saved = section_args
        tables = make_tables(route_ids.reshape(N_EP, TOK_DEV, TOP))

        def shard_partial(shard_index):
            grad_pre = lax.optimization_barrier(swiglu_backward(jnp.take(upstream, shard_index, axis=0), jnp.take(saved, shard_index, axis=0)))
            shard_weights = jnp.take(weights, shard_index, axis=0).astype(jnp.float32)
            product = jnp.einsum('sch,dh->scd', grad_pre.astype(jnp.float32), shard_weights)
            return lax.optimization_barrier(product.astype(jnp.bfloat16))

        def one_expert(running, expert):
            leading = shard_partial(2 * expert).astype(jnp.float32)
            trailing = shard_partial(2 * expert + 1).astype(jnp.float32)
            pair_sum = lax.optimization_barrier((leading + trailing).astype(jnp.bfloat16)).astype(jnp.float32)
            expert_table = jnp.take(tables, expert, axis=1)
            return running + jnp.einsum('sct,scd->std', expert_table, pair_sum), None

        accumulated, _ = lax.scan(one_expert, jnp.zeros((N_EP, TOK_DEV, D), jnp.float32), jnp.arange(EXPERTS, dtype=jnp.int32))
        return accumulated.astype(jnp.bfloat16).reshape(N_EP * TOK_DEV, D)

    grad_in = lax.map(section_backward, (bwd_experts, expert_weights, grad_hidden, saved_pre))
    return hidden_out, jnp.roll(grad_in, -1, axis=0)
```

```python
import jax
import jax.numpy as jnp
from jax import lax
from jax.sharding import PartitionSpec as P

PARTS = 2


def shifted(block, axis, distance):
    devices = range(lax.axis_size(axis))
    route = [((i - distance) % len(devices), i) for i in devices]
    return lax.ppermute(block, axis, route)


def partner_of(value):
    pairs = [(i, i ^ 1) for i in range(lax.axis_size("ep"))]
    return lax.ppermute(value, "ep", pairs)


def step_along(value, first, last, way):
    pairs = [(2 * z + c, 2 * (z + way) + c) for z in range(first, last + 1) for c in range(2)]
    return lax.ppermute(value, "ep", pairs)


def slots_of(route_ids, expert, capacity):
    named = jnp.any(route_ids == expert, axis=2).astype(jnp.int32)
    slot = jnp.cumsum(named, axis=1) - 1
    place = jnp.where(named == 1, slot, -1)
    return (place[:, None, :] == jnp.arange(capacity, dtype=jnp.int32)[None, :, None]).astype(
        jnp.bfloat16
    )


def swiglu_backward(upstream, saved):
    hid_units = upstream.shape[-1]
    pre_float = saved.astype(jnp.float32)
    gate_pre = pre_float[..., :hid_units]
    up_pre = pre_float[..., hid_units:]
    sigmoid_gate = jax.nn.sigmoid(gate_pre)
    upstream_float = upstream.astype(jnp.float32)
    grad_gate = upstream_float * up_pre * sigmoid_gate * (1.0 + gate_pre * (1.0 - sigmoid_gate))
    grad_up = upstream_float * gate_pre * sigmoid_gate
    return jnp.concatenate([grad_gate, grad_up], axis=-1).astype(jnp.bfloat16)


def shards(prev_out, fwd_experts, expert_weights, bwd_experts, grad_hidden, saved_pre):
    groups = lax.axis_size("ep")
    chips = groups // 2
    capacity = grad_hidden.shape[3]
    hid_units = grad_hidden.shape[4]
    width = prev_out.shape[2]
    part = width // PARTS
    weights = expert_weights[0, 0]
    me = lax.axis_index("ep")
    z, core = me // 2, me % 2
    tokens, top = fwd_experts.shape[1:]

    routes = lax.all_gather(
        jnp.concatenate([fwd_experts[0], bwd_experts[0]], axis=1), "ep", axis=0
    )
    fwd_pick = slots_of(routes[..., :top], z, capacity)
    bwd_pick = slots_of(routes[..., top:], z, capacity)
    fwd_own = lax.dynamic_index_in_dim(
        fwd_pick.reshape(chips, 2, capacity, tokens), core, 1, keepdims=False
    )
    bwd_own = lax.dynamic_index_in_dim(
        bwd_pick.reshape(chips, 2, capacity, tokens), core, 1, keepdims=False
    )

    grad_pre = swiglu_backward(grad_hidden[0, 0], saved_pre[0, 0])
    by_core = grad_pre.reshape(chips, 2, capacity, 2 * hid_units)
    grad_own = lax.dynamic_index_in_dim(by_core, core, 1, keepdims=False)
    grad_other = lax.dynamic_index_in_dim(by_core, 1 - core, 1, keepdims=False)

    projected_own = 0.0
    projected_other = 0.0
    grad_rows = []
    for k in range(PARTS):
        columns = slice(k * part, (k + 1) * part)
        own_weights = weights[columns]

        rows = shifted(prev_out[0, :, columns], "pp", 1)
        below, above = [], []
        up = down = rows
        for hop in range(1, chips):
            up = step_along(up, hop - 1, chips - 2, 1)
            down = step_along(down, 1, chips - hop, -1)
            below.insert(0, up)
            above.append(down)
        line = jnp.stack(below + [rows] + above)
        line = lax.dynamic_slice_in_dim(line, chips - 1 - z, chips, 0)
        picked = jnp.einsum(
            "nct,ntd->ncd", fwd_own, line, preferred_element_type=jnp.float32
        ).astype(jnp.bfloat16)
        picked_other = partner_of(picked)
        projected_own += jnp.einsum(
            "ncd,dh->nch", picked, own_weights, preferred_element_type=jnp.float32
        )
        projected_other += jnp.einsum(
            "ncd,dh->nch", picked_other, own_weights, preferred_element_type=jnp.float32
        )

        partial_other = jnp.einsum(
            "nch,dh->ncd", grad_other, own_weights, preferred_element_type=jnp.float32
        ).astype(jnp.bfloat16)
        received = partner_of(partial_other)
        partial_own = jnp.einsum(
            "nch,dh->ncd", grad_own, own_weights, preferred_element_type=jnp.float32
        ).astype(jnp.bfloat16)
        pair = (partial_own.astype(jnp.float32) + received.astype(jnp.float32)).astype(
            jnp.bfloat16
        )
        terms = jnp.einsum(
            "nct,ncd->ntd", bwd_own, pair, preferred_element_type=jnp.float32
        ).astype(jnp.bfloat16)
        up = down = 0.0
        for hop in range(1, chips):
            above_term = lax.dynamic_index_in_dim(
                terms, jnp.minimum(z + chips - hop, chips - 1), 0, keepdims=False
            )
            below_term = lax.dynamic_index_in_dim(
                terms, jnp.maximum(z - chips + hop, 0), 0, keepdims=False
            )
            up = step_along((above_term + up).astype(jnp.bfloat16), 0, hop - 1, 1)
            down = step_along((below_term + down).astype(jnp.bfloat16), chips - hop, chips - 1, -1)
        mine = lax.dynamic_index_in_dim(terms, z, 0, keepdims=False)
        grad_in = (
            mine.astype(jnp.float32) + up.astype(jnp.float32) + down.astype(jnp.float32)
        ).astype(jnp.bfloat16)
        grad_rows.append(shifted(grad_in, "pp", -1))

    def activated(projected):
        return (jax.nn.silu(projected[..., :hid_units]) * projected[..., hid_units:]).astype(
            jnp.bfloat16
        )

    own, other = activated(projected_own), activated(projected_other)
    hidden = jnp.stack(
        [jnp.where(core == 0, own, other), jnp.where(core == 0, other, own)], axis=1
    ).reshape(groups, capacity, hid_units)
    return hidden[None, None], jnp.concatenate(grad_rows, axis=1)[None]


def solution(mesh):
    placed = (
        P("pp", "ep", None),
        P("pp", "ep", None),
        P("pp", "ep", None, None),
        P("pp", "ep", None),
        P("pp", "ep", None, None, None),
        P("pp", "ep", None, None, None),
    )
    return jax.shard_map(
        shards,
        mesh=mesh,
        in_specs=placed,
        out_specs=(P("pp", "ep", None, None, None), P("pp", "ep", None)),
        check_vma=False,
    )
```

```python
import functools

import jax
import jax.numpy as jnp
from jax import lax
from jax.experimental import pallas as pl
from jax.experimental.pallas import tpu as pltpu
from jax.sharding import PartitionSpec as P

PARTS = 2
CHUNK = 1024
TILE = 256
RESIDENT = 40 * 2**20
F32 = jnp.float32
BF16 = jnp.bfloat16


def shifted(block, axis, distance):
    devices = range(lax.axis_size(axis))
    route = [((i - distance) % len(devices), i) for i in devices]
    return lax.ppermute(block, axis, route)


def partner_of(value):
    pairs = [(i, i ^ 1) for i in range(lax.axis_size("ep"))]
    return lax.ppermute(value, "ep", pairs)


def step_along(value, first, last, way):
    pairs = [(2 * z + c, 2 * (z + way) + c) for z in range(first, last + 1) for c in range(2)]
    return lax.ppermute(value, "ep", pairs)


def slots_of(route_ids, expert, capacity):
    named = jnp.any(route_ids == expert, axis=2).astype(jnp.int32)
    slot = jnp.cumsum(named, axis=1) - 1
    place = jnp.where(named == 1, slot, -1)
    return (place[:, None, :] == jnp.arange(capacity, dtype=jnp.int32)[None, :, None]).astype(
        jnp.bfloat16
    )


def swiglu_backward(upstream, saved):
    hid_units = upstream.shape[-1]
    pre_float = saved.astype(jnp.float32)
    gate_pre = pre_float[..., :hid_units]
    up_pre = pre_float[..., hid_units:]
    sigmoid_gate = jax.nn.sigmoid(gate_pre)
    upstream_float = upstream.astype(jnp.float32)
    grad_gate = upstream_float * up_pre * sigmoid_gate * (1.0 + gate_pre * (1.0 - sigmoid_gate))
    grad_up = upstream_float * gate_pre * sigmoid_gate
    return jnp.concatenate([grad_gate, grad_up], axis=-1).astype(jnp.bfloat16)


def permute_form(prev_out, fwd_experts, expert_weights, bwd_experts, grad_hidden, saved_pre):
    groups = lax.axis_size("ep")
    chips = groups // 2
    capacity = grad_hidden.shape[3]
    hid_units = grad_hidden.shape[4]
    width = prev_out.shape[2]
    part = width // PARTS
    weights = expert_weights[0, 0]
    me = lax.axis_index("ep")
    z, core = me // 2, me % 2
    tokens, top = fwd_experts.shape[1:]

    routes = lax.all_gather(
        jnp.concatenate([fwd_experts[0], bwd_experts[0]], axis=1), "ep", axis=0
    )
    fwd_pick = slots_of(routes[..., :top], z, capacity)
    bwd_pick = slots_of(routes[..., top:], z, capacity)
    fwd_own = lax.dynamic_index_in_dim(
        fwd_pick.reshape(chips, 2, capacity, tokens), core, 1, keepdims=False
    )
    bwd_own = lax.dynamic_index_in_dim(
        bwd_pick.reshape(chips, 2, capacity, tokens), core, 1, keepdims=False
    )

    grad_pre = swiglu_backward(grad_hidden[0, 0], saved_pre[0, 0])
    by_core = grad_pre.reshape(chips, 2, capacity, 2 * hid_units)
    grad_own = lax.dynamic_index_in_dim(by_core, core, 1, keepdims=False)
    grad_other = lax.dynamic_index_in_dim(by_core, 1 - core, 1, keepdims=False)

    projected_own = 0.0
    projected_other = 0.0
    grad_rows = []
    for k in range(PARTS):
        columns = slice(k * part, (k + 1) * part)
        own_weights = weights[columns]

        rows = shifted(prev_out[0, :, columns], "pp", 1)
        below, above = [], []
        up = down = rows
        for hop in range(1, chips):
            up = step_along(up, hop - 1, chips - 2, 1)
            down = step_along(down, 1, chips - hop, -1)
            below.insert(0, up)
            above.append(down)
        line = jnp.stack(below + [rows] + above)
        line = lax.dynamic_slice_in_dim(line, chips - 1 - z, chips, 0)
        picked = jnp.einsum(
            "nct,ntd->ncd", fwd_own, line, preferred_element_type=jnp.float32
        ).astype(jnp.bfloat16)
        picked_other = partner_of(picked)
        projected_own += jnp.einsum(
            "ncd,dh->nch", picked, own_weights, preferred_element_type=jnp.float32
        )
        projected_other += jnp.einsum(
            "ncd,dh->nch", picked_other, own_weights, preferred_element_type=jnp.float32
        )

        partial_other = jnp.einsum(
            "nch,dh->ncd", grad_other, own_weights, preferred_element_type=jnp.float32
        ).astype(jnp.bfloat16)
        received = partner_of(partial_other)
        partial_own = jnp.einsum(
            "nch,dh->ncd", grad_own, own_weights, preferred_element_type=jnp.float32
        ).astype(jnp.bfloat16)
        pair = (partial_own.astype(jnp.float32) + received.astype(jnp.float32)).astype(
            jnp.bfloat16
        )
        terms = jnp.einsum(
            "nct,ncd->ntd", bwd_own, pair, preferred_element_type=jnp.float32
        ).astype(jnp.bfloat16)
        up = down = 0.0
        for hop in range(1, chips):
            above_term = lax.dynamic_index_in_dim(
                terms, jnp.minimum(z + chips - hop, chips - 1), 0, keepdims=False
            )
            below_term = lax.dynamic_index_in_dim(
                terms, jnp.maximum(z - chips + hop, 0), 0, keepdims=False
            )
            up = step_along((above_term + up).astype(jnp.bfloat16), 0, hop - 1, 1)
            down = step_along((below_term + down).astype(jnp.bfloat16), chips - hop, chips - 1, -1)
        mine = lax.dynamic_index_in_dim(terms, z, 0, keepdims=False)
        grad_in = (
            mine.astype(jnp.float32) + up.astype(jnp.float32) + down.astype(jnp.float32)
        ).astype(jnp.bfloat16)
        grad_rows.append(shifted(grad_in, "pp", -1))

    def activated(projected):
        return (jax.nn.silu(projected[..., :hid_units]) * projected[..., hid_units:]).astype(
            jnp.bfloat16
        )

    own, other = activated(projected_own), activated(projected_other)
    hidden = jnp.stack(
        [jnp.where(core == 0, own, other), jnp.where(core == 0, other, own)], axis=1
    ).reshape(groups, capacity, hid_units)
    return hidden[None, None], jnp.concatenate(grad_rows, axis=1)[None]


def dot(a, b, dims):
    return lax.dot_general(a, b, (dims, ((), ())), preferred_element_type=F32)


def relay_kernel(
    chunk, routes, prev_out, weights, upstream, saved, hidden, grad_rows,
    rows, terms, landed, picked, picked_in, part_out, part_own, part_in, result,
    total, grad_pre, w_fwd, w_bwd, tables, pick_fwd, pick_bwd,
    shift_send, rows_recv, rows_send, land_recv, land_send, back_send, back_recv,
    picked_send, picked_recv, part_send, part_recv, wf_sem, wb_sem, table_send, table_recv,
):
    chips, _, capacity, hid_units = upstream.shape
    tokens, width = prev_out.shape
    count = width // chunk
    tiles = chunk // TILE
    sections = lax.axis_size("pp")
    me, section = lax.axis_index("ep"), lax.axis_index("pp")
    z, core = me // 2, me % 2
    other = 1 - core
    partner = {"ep": 2 * z + other}
    above = {"ep": jnp.minimum(me + 2, 2 * chips - 1)}
    below = {"ep": jnp.maximum(me - 2, 0)}
    after = {"pp": lax.rem(section + 1, sections)}
    before = {"pp": lax.rem(section + sections - 1, sections)}
    last = chips - 1

    def remote(src, dst, send, recv, device):
        return pltpu.make_async_remote_copy(
            src_ref=src, dst_ref=dst, send_sem=send, recv_sem=recv,
            device_id=device, device_id_type=pl.DeviceIdType.MESH,
        )

    def columns(k):
        return pl.ds(pl.multiple_of(k * chunk, chunk), chunk)

    def tile(i):
        return pl.ds(pl.multiple_of(i * TILE, TILE), TILE)

    def shift(k):
        return remote(
            prev_out.at[:, columns(k)], rows.at[k, z], shift_send.at[k], rows_recv.at[k, z], after
        )

    def row_up(k, o):
        return remote(rows.at[k, o], rows.at[k, o], rows_send.at[k, o], rows_recv.at[k, o], above)

    def row_down(k, o):
        slot = jnp.where(o == z, chips, o)
        return remote(
            rows.at[k, o], rows.at[k, o], rows_send.at[k, slot], rows_recv.at[k, o], below
        )

    def sum_up(k, d):
        return remote(
            terms.at[k, d], landed.at[k, d], land_send.at[k, d], land_recv.at[k, d], above
        )

    def sum_down(k, d):
        slot = jnp.where(d == z - 1, chips, d)
        return remote(
            terms.at[k, d], landed.at[k, slot], land_send.at[k, d], land_recv.at[k, slot], below
        )

    def landing(k, slot):
        return remote(
            terms.at[k, 0], landed.at[k, slot], land_send.at[k, 0], land_recv.at[k, slot], partner
        )

    def back(k):
        return remote(
            result.at[k], grad_rows.at[:, columns(k)], back_send.at[k], back_recv.at[k], before
        )

    def part_copy(k):
        s = lax.rem(k, 2)
        return remote(part_out.at[s], part_in.at[s], part_send.at[s], part_recv.at[s], partner)

    def picked_copy(k):
        s = lax.rem(k, 2)
        return remote(
            picked.at[s], picked_in.at[s], picked_send.at[s], picked_recv.at[s], partner
        )

    def table_copy(o):
        return remote(
            tables.at[z], tables.at[z], table_send.at[o], table_recv.at[z], {"ep": 2 * o + core}
        )

    def load_fwd(k):
        s = lax.rem(k, 2)
        return pltpu.make_async_copy(weights.at[columns(k)], w_fwd.at[s], wf_sem.at[s])

    def load_bwd(k):
        s = lax.rem(k, 2)
        return pltpu.make_async_copy(weights.at[columns(k)], w_bwd.at[s], wb_sem.at[s])

    load_bwd(0).start()
    load_fwd(0).start()

    barrier = pltpu.get_barrier_semaphore()
    for device in (partner, after, before):
        pl.semaphore_signal(barrier, 1, device_id=device, device_id_type=pl.DeviceIdType.MESH)
    for o in range(chips):
        @pl.when(o != z)
        def _():
            pl.semaphore_signal(
                barrier, 1, device_id={"ep": 2 * o + core}, device_id_type=pl.DeviceIdType.MESH
            )

    experts = lax.broadcasted_iota(jnp.int32, (chips, tokens), 0)
    named = jnp.concatenate(
        [
            jnp.where(
                (routes[2 * i : 2 * i + 1, :] == experts)
                | (routes[2 * i + 1 : 2 * i + 2, :] == experts),
                1.0,
                0.0,
            )
            for i in range(2)
        ],
        axis=0,
    ).astype(F32)
    upto = jnp.where(
        lax.broadcasted_iota(jnp.int32, (tokens, tokens), 0)
        <= lax.broadcasted_iota(jnp.int32, (tokens, tokens), 1),
        1.0,
        0.0,
    ).astype(BF16)
    ordinal = dot(named.astype(BF16), upto, ((1,), (0,)))
    tables[z] = jnp.where(named > 0.5, ordinal - 1.0, -1.0)

    pl.semaphore_wait(barrier, 3 + last)
    for o in range(chips):
        @pl.when(o != z)
        def _():
            table_copy(o).start()
    lax.fori_loop(0, count, lambda k, c: (shift(k).start(), c)[1], 0)

    for parity, source in ((0, core), (1, other)):
        @pl.loop(0, chips)
        def _(o):
            gate = saved[o, source, :, :hid_units].astype(F32)
            up = saved[o, source, :, hid_units:].astype(F32)
            grad = upstream[o, source].astype(F32)
            sig = 1.0 / (1.0 + jnp.exp(-gate))
            grad_pre[parity, o, :, :hid_units] = (
                grad * up * sig * (1.0 + gate * (1.0 - sig))
            ).astype(BF16)
            grad_pre[parity, o, :, hid_units:] = (grad * gate * sig).astype(BF16)

    total[...] = jnp.zeros_like(total)

    for o in range(chips):
        @pl.when(o != z)
        def _():
            remote(
                tables.at[o], tables.at[o], table_send.at[o], table_recv.at[o], partner
            ).wait_recv()
    slots = lax.broadcasted_iota(jnp.int32, (capacity, tokens), 0).astype(F32)
    for o in range(chips):
        pick_fwd[o] = jnp.where(tables[o, pl.ds(z, 1), :] == slots, 1.0, 0.0).astype(BF16)
        pick_bwd[o] = jnp.where(tables[o, pl.ds(chips + z, 1), :] == slots, 1.0, 0.0).astype(BF16)

    def partial_rows(parity, s, target):
        @pl.loop(0, tiles)
        def _(i):
            grads = grad_pre[parity].reshape(chips * capacity, 2 * hid_units)
            product = dot(grads, w_bwd[s, tile(i), :], ((1,), (1,)))
            target[:, :, tile(i)] = product.astype(BF16).reshape(chips, capacity, TILE)

    def project(which, source, s):
        @pl.loop(0, 2 * hid_units // TILE)
        def _(i):
            data = source[...].reshape(chips * capacity, chunk)
            total[which, :, tile(i)] += dot(data, w_fwd[s, :, tile(i)], ((1,), (0,)))

    def add_landed(k, d):
        terms[k, d] = (terms[k, d].astype(F32) + landed[k, d].astype(F32)).astype(BF16)

    def step(t, carry):
        @pl.when(t < count)
        def _():
            s = lax.rem(t, 2)
            load_bwd(t).wait()

            @pl.when(t + 1 < count)
            def _():
                load_bwd(t + 1).start()

            @pl.when(t >= 2)
            def _():
                part_copy(t).wait_send()

            partial_rows(1, s, part_out.at[s])
            part_copy(t).start()
            shift(t).wait_recv()

            @pl.when(z < last)
            def _():
                row_up(t, z).start()

            @pl.when(z > 0)
            def _():
                row_down(t, z).start()

            partial_rows(0, s, part_own)
            part_copy(t).wait_recv()

            @pl.loop(0, chips)
            def _(o):
                @pl.loop(0, tiles)
                def _(i):
                    pair = (
                        part_own[o, :, tile(i)].astype(F32) + part_in[s, o, :, tile(i)].astype(F32)
                    ).astype(BF16)
                    terms[t, o, :, tile(i)] = dot(pick_bwd[o], pair, ((0,), (0,))).astype(BF16)

        up_k = t - z

        @pl.when((up_k >= 0) & (up_k < count) & (z < last))
        def _():
            for d in range(last, 0, -1):
                @pl.when(d > z)
                def _():
                    @pl.when(z > 0)
                    def _():
                        landing(up_k, d).wait_recv()
                        add_landed(up_k, d)

                    sum_up(up_k, d).start()

        down_k = t - (last - z)

        @pl.when((down_k >= 0) & (down_k < count) & (z > 0))
        def _():
            for d in range(last):
                @pl.when(d < z)
                def _():
                    @pl.when(z < last)
                    def _():
                        landing(down_k, d).wait_recv()
                        add_landed(down_k, d)

                    sum_down(down_k, d).start()

        for hop in range(1, chips):
            k = t - hop

            @pl.when((k >= 0) & (k < count))
            def _():
                @pl.when(z >= hop)
                def _():
                    o = jnp.maximum(z - hop, 0)
                    row_up(k, o).wait_recv()

                    @pl.when(z < last)
                    def _():
                        row_up(k, o).start()

                @pl.when(z + hop <= last)
                def _():
                    o = jnp.minimum(z + hop, last)
                    row_down(k, o).wait_recv()

                    @pl.when(z > 0)
                    def _():
                        row_down(k, o).start()

        end_k = t - last

        @pl.when((end_k >= 0) & (end_k < count))
        def _():
            result[end_k] = terms[end_k, z]

            @pl.when(z > 0)
            def _():
                landing(end_k, z).wait_recv()
                result[end_k] = (
                    result[end_k].astype(F32) + landed[end_k, z].astype(F32)
                ).astype(BF16)

            @pl.when(z < last)
            def _():
                landing(end_k, chips).wait_recv()
                result[end_k] = (
                    result[end_k].astype(F32) + landed[end_k, chips].astype(F32)
                ).astype(BF16)

            back(end_k).start()

        mul_k = t - chips

        @pl.when((mul_k >= 0) & (mul_k < count))
        def _():
            s = lax.rem(mul_k, 2)
            load_fwd(mul_k).wait()

            @pl.when(mul_k + 1 < count)
            def _():
                load_fwd(mul_k + 1).start()

            project(0, picked.at[s], s)
            picked_copy(mul_k).wait()
            project(1, picked_in.at[s], s)

        @pl.when((end_k >= 0) & (end_k < count))
        def _():
            s = lax.rem(end_k, 2)

            @pl.loop(0, chips)
            def _(o):
                @pl.loop(0, tiles)
                def _(i):
                    picked[s, o, :, tile(i)] = dot(
                        pick_fwd[o], rows[end_k, o, :, tile(i)], ((1,), (0,))
                    ).astype(BF16)

            picked_copy(end_k).start()

        return carry

    lax.fori_loop(0, count + chips, step, 0)

    for parity, source in ((0, core), (1, other)):
        @pl.loop(0, chips)
        def _(o):
            block = pl.ds(pl.multiple_of(o * capacity, capacity), capacity)
            gate = total[parity, block, :hid_units]
            up = total[parity, block, hid_units:]
            hidden[o, source] = (gate / (1.0 + jnp.exp(-gate)) * up).astype(BF16)

    def finish(k, carry):
        shift(k).wait_send()
        back(k).wait()
        for o in range(chips):
            @pl.when((o <= z) & (z < last))
            def _():
                row_up(k, o).wait_send()

            @pl.when((o >= z) & (z > 0))
            def _():
                row_down(k, o).wait_send()

            @pl.when(o != z)
            def _():
                sum_up(k, o).wait_send()

        return carry

    lax.fori_loop(0, count, finish, 0)
    for k in range(max(count - 2, 0), count):
        part_copy(k).wait_send()
    for o in range(chips):
        @pl.when(o != z)
        def _():
            table_copy(o).wait_send()


def kernel_form(prev_out, fwd_experts, expert_weights, bwd_experts, grad_hidden, saved_pre):
    groups, capacity, hid_units = grad_hidden.shape[2:]
    chips = groups // 2
    tokens, width = prev_out.shape[1:]
    chunk = CHUNK
    count = width // chunk
    routes = jnp.concatenate([fwd_experts[0], bwd_experts[0]], axis=1).T
    hbm = pl.BlockSpec(memory_space=pl.ANY)
    vmem = pl.BlockSpec(memory_space=pltpu.VMEM)
    dma = pltpu.SemaphoreType.DMA
    slots = chips * capacity
    hidden, grad_rows = pl.pallas_call(
        functools.partial(relay_kernel, chunk),
        out_shape=(
            jax.ShapeDtypeStruct((chips, 2, capacity, hid_units), BF16),
            jax.ShapeDtypeStruct((tokens, width), BF16),
        ),
        in_specs=[vmem, hbm, hbm, vmem, vmem],
        out_specs=(vmem, hbm),
        scratch_shapes=[
            pltpu.VMEM((count, chips, tokens, chunk), BF16),
            pltpu.VMEM((count, chips, tokens, chunk), BF16),
            pltpu.VMEM((count, chips + 1, tokens, chunk), BF16),
            pltpu.VMEM((2, chips, capacity, chunk), BF16),
            pltpu.VMEM((2, chips, capacity, chunk), BF16),
            pltpu.VMEM((2, chips, capacity, chunk), BF16),
            pltpu.VMEM((chips, capacity, chunk), BF16),
            pltpu.VMEM((2, chips, capacity, chunk), BF16),
            pltpu.VMEM((count, tokens, chunk), BF16),
            pltpu.VMEM((2, slots, 2 * hid_units), F32),
            pltpu.VMEM((2, chips, capacity, 2 * hid_units), BF16),
            pltpu.VMEM((2, chunk, 2 * hid_units), BF16),
            pltpu.VMEM((2, chunk, 2 * hid_units), BF16),
            pltpu.VMEM((chips, 2 * chips, tokens), F32),
            pltpu.VMEM((chips, capacity, tokens), BF16),
            pltpu.VMEM((chips, capacity, tokens), BF16),
            dma((count,)),
            dma((count, chips)),
            dma((count, chips + 1)),
            dma((count, chips + 1)),
            dma((count, chips)),
            dma((count,)),
            dma((count,)),
            dma((2,)),
            dma((2,)),
            dma((2,)),
            dma((2,)),
            dma((2,)),
            dma((2,)),
            dma((chips,)),
            dma((chips,)),
        ],
        compiler_params=pltpu.CompilerParams(
            collective_id=0, has_side_effects=True, vmem_limit_bytes=60 * 2**20
        ),
        cost_estimate=pl.CostEstimate(
            flops=8 * groups * capacity * width * hid_units,
            bytes_accessed=4 * width * hid_units,
            transcendentals=2 * groups * capacity * hid_units,
        ),
        name="relay",
    )(
        routes,
        prev_out[0],
        expert_weights[0, 0],
        grad_hidden.reshape(chips, 2, capacity, hid_units),
        saved_pre.reshape(chips, 2, capacity, 2 * hid_units),
    )
    return hidden.reshape(grad_hidden.shape), grad_rows[None]


def shards(prev_out, *rest):
    chips = lax.axis_size("ep") // 2
    held = 3 * chips * prev_out.shape[1] * prev_out.shape[2] * 2
    form = kernel_form if held <= RESIDENT and prev_out.shape[2] % CHUNK == 0 else permute_form
    return form(prev_out, *rest)


def solution(mesh):
    placed = (
        P("pp", "ep", None),
        P("pp", "ep", None),
        P("pp", "ep", None, None),
        P("pp", "ep", None),
        P("pp", "ep", None, None, None),
        P("pp", "ep", None, None, None),
    )
    return jax.shard_map(
        shards,
        mesh=mesh,
        in_specs=placed,
        out_specs=(P("pp", "ep", None, None, None), P("pp", "ep", None)),
        check_vma=False,
    )
```

```python
import functools

import jax
import jax.numpy as jnp
from jax import lax
from jax.experimental import pallas as pl
from jax.experimental.pallas import tpu as pltpu
from jax.sharding import PartitionSpec as P

PARTS = 2
CHUNK = 512
TILE = 256
RESIDENT = 40 * 2**20
F32 = jnp.float32
BF16 = jnp.bfloat16


def shifted(block, axis, distance):
    devices = range(lax.axis_size(axis))
    route = [((i - distance) % len(devices), i) for i in devices]
    return lax.ppermute(block, axis, route)


def partner_of(value):
    pairs = [(i, i ^ 1) for i in range(lax.axis_size("ep"))]
    return lax.ppermute(value, "ep", pairs)


def step_along(value, first, last, way):
    pairs = [(2 * z + c, 2 * (z + way) + c) for z in range(first, last + 1) for c in range(2)]
    return lax.ppermute(value, "ep", pairs)


def slots_of(route_ids, expert, capacity):
    named = jnp.any(route_ids == expert, axis=2).astype(jnp.int32)
    slot = jnp.cumsum(named, axis=1) - 1
    place = jnp.where(named == 1, slot, -1)
    return (place[:, None, :] == jnp.arange(capacity, dtype=jnp.int32)[None, :, None]).astype(
        jnp.bfloat16
    )


def swiglu_backward(upstream, saved):
    hid_units = upstream.shape[-1]
    pre_float = saved.astype(jnp.float32)
    gate_pre = pre_float[..., :hid_units]
    up_pre = pre_float[..., hid_units:]
    sigmoid_gate = jax.nn.sigmoid(gate_pre)
    upstream_float = upstream.astype(jnp.float32)
    grad_gate = upstream_float * up_pre * sigmoid_gate * (1.0 + gate_pre * (1.0 - sigmoid_gate))
    grad_up = upstream_float * gate_pre * sigmoid_gate
    return jnp.concatenate([grad_gate, grad_up], axis=-1).astype(jnp.bfloat16)


def permute_form(prev_out, fwd_experts, expert_weights, bwd_experts, grad_hidden, saved_pre):
    groups = lax.axis_size("ep")
    chips = groups // 2
    capacity = grad_hidden.shape[3]
    hid_units = grad_hidden.shape[4]
    width = prev_out.shape[2]
    part = width // PARTS
    weights = expert_weights[0, 0]
    me = lax.axis_index("ep")
    z, core = me // 2, me % 2
    tokens, top = fwd_experts.shape[1:]

    routes = lax.all_gather(
        jnp.concatenate([fwd_experts[0], bwd_experts[0]], axis=1), "ep", axis=0
    )
    fwd_pick = slots_of(routes[..., :top], z, capacity)
    bwd_pick = slots_of(routes[..., top:], z, capacity)
    fwd_own = lax.dynamic_index_in_dim(
        fwd_pick.reshape(chips, 2, capacity, tokens), core, 1, keepdims=False
    )
    bwd_own = lax.dynamic_index_in_dim(
        bwd_pick.reshape(chips, 2, capacity, tokens), core, 1, keepdims=False
    )

    grad_pre = swiglu_backward(grad_hidden[0, 0], saved_pre[0, 0])
    by_core = grad_pre.reshape(chips, 2, capacity, 2 * hid_units)
    grad_own = lax.dynamic_index_in_dim(by_core, core, 1, keepdims=False)
    grad_other = lax.dynamic_index_in_dim(by_core, 1 - core, 1, keepdims=False)

    projected_own = 0.0
    projected_other = 0.0
    grad_rows = []
    for k in range(PARTS):
        columns = slice(k * part, (k + 1) * part)
        own_weights = weights[columns]

        rows = shifted(prev_out[0, :, columns], "pp", 1)
        below, above = [], []
        up = down = rows
        for hop in range(1, chips):
            up = step_along(up, hop - 1, chips - 2, 1)
            down = step_along(down, 1, chips - hop, -1)
            below.insert(0, up)
            above.append(down)
        line = jnp.stack(below + [rows] + above)
        line = lax.dynamic_slice_in_dim(line, chips - 1 - z, chips, 0)
        picked = jnp.einsum(
            "nct,ntd->ncd", fwd_own, line, preferred_element_type=jnp.float32
        ).astype(jnp.bfloat16)
        picked_other = partner_of(picked)
        projected_own += jnp.einsum(
            "ncd,dh->nch", picked, own_weights, preferred_element_type=jnp.float32
        )
        projected_other += jnp.einsum(
            "ncd,dh->nch", picked_other, own_weights, preferred_element_type=jnp.float32
        )

        partial_other = jnp.einsum(
            "nch,dh->ncd", grad_other, own_weights, preferred_element_type=jnp.float32
        ).astype(jnp.bfloat16)
        received = partner_of(partial_other)
        partial_own = jnp.einsum(
            "nch,dh->ncd", grad_own, own_weights, preferred_element_type=jnp.float32
        ).astype(jnp.bfloat16)
        pair = (partial_own.astype(jnp.float32) + received.astype(jnp.float32)).astype(
            jnp.bfloat16
        )
        terms = jnp.einsum(
            "nct,ncd->ntd", bwd_own, pair, preferred_element_type=jnp.float32
        ).astype(jnp.bfloat16)
        up = down = 0.0
        for hop in range(1, chips):
            above_term = lax.dynamic_index_in_dim(
                terms, jnp.minimum(z + chips - hop, chips - 1), 0, keepdims=False
            )
            below_term = lax.dynamic_index_in_dim(
                terms, jnp.maximum(z - chips + hop, 0), 0, keepdims=False
            )
            up = step_along((above_term + up).astype(jnp.bfloat16), 0, hop - 1, 1)
            down = step_along((below_term + down).astype(jnp.bfloat16), chips - hop, chips - 1, -1)
        mine = lax.dynamic_index_in_dim(terms, z, 0, keepdims=False)
        grad_in = (
            mine.astype(jnp.float32) + up.astype(jnp.float32) + down.astype(jnp.float32)
        ).astype(jnp.bfloat16)
        grad_rows.append(shifted(grad_in, "pp", -1))

    def activated(projected):
        return (jax.nn.silu(projected[..., :hid_units]) * projected[..., hid_units:]).astype(
            jnp.bfloat16
        )

    own, other = activated(projected_own), activated(projected_other)
    hidden = jnp.stack(
        [jnp.where(core == 0, own, other), jnp.where(core == 0, other, own)], axis=1
    ).reshape(groups, capacity, hid_units)
    return hidden[None, None], jnp.concatenate(grad_rows, axis=1)[None]


def dot(a, b, dims):
    return lax.dot_general(a, b, (dims, ((), ())), preferred_element_type=F32)


def relay_kernel(
    chunk, routes, prev_out, weights, upstream, saved, hidden, grad_rows,
    rows, terms, landed, picked, picked_in, part_out, part_own, part_in, result,
    total, grad_pre, w_fwd, w_bwd, tables, pick_fwd, pick_bwd,
    shift_send, rows_recv, rows_send, land_recv, land_send, back_send, back_recv,
    picked_send, picked_recv, part_send, part_recv, wf_sem, wb_sem, table_send, table_recv,
):
    chips, _, capacity, hid_units = upstream.shape
    tokens, width = prev_out.shape
    count = width // chunk
    tiles = chunk // TILE
    sections = lax.axis_size("pp")
    me, section = lax.axis_index("ep"), lax.axis_index("pp")
    z, core = me // 2, me % 2
    other = 1 - core
    partner = {"ep": 2 * z + other}
    above = {"ep": jnp.minimum(me + 2, 2 * chips - 1)}
    below = {"ep": jnp.maximum(me - 2, 0)}
    after = {"pp": lax.rem(section + 1, sections)}
    before = {"pp": lax.rem(section + sections - 1, sections)}
    last = chips - 1

    def remote(src, dst, send, recv, device):
        return pltpu.make_async_remote_copy(
            src_ref=src, dst_ref=dst, send_sem=send, recv_sem=recv,
            device_id=device, device_id_type=pl.DeviceIdType.MESH,
        )

    def columns(k):
        return pl.ds(pl.multiple_of(k * chunk, chunk), chunk)

    def tile(i):
        return pl.ds(pl.multiple_of(i * TILE, TILE), TILE)

    def shift(k):
        return remote(
            prev_out.at[:, columns(k)], rows.at[k, z], shift_send.at[k], rows_recv.at[k, z], after
        )

    def row_up(k, o):
        return remote(rows.at[k, o], rows.at[k, o], rows_send.at[k, o], rows_recv.at[k, o], above)

    def row_down(k, o):
        slot = jnp.where(o == z, chips, o)
        return remote(
            rows.at[k, o], rows.at[k, o], rows_send.at[k, slot], rows_recv.at[k, o], below
        )

    def sum_up(k, d):
        return remote(
            terms.at[k, d], landed.at[k, d], land_send.at[k, d], land_recv.at[k, d], above
        )

    def sum_down(k, d):
        slot = jnp.where(d == z - 1, chips, d)
        return remote(
            terms.at[k, d], landed.at[k, slot], land_send.at[k, d], land_recv.at[k, slot], below
        )

    def landing(k, slot):
        return remote(
            terms.at[k, 0], landed.at[k, slot], land_send.at[k, 0], land_recv.at[k, slot], partner
        )

    def back(k):
        return remote(
            result.at[k], grad_rows.at[:, columns(k)], back_send.at[k], back_recv.at[k], before
        )

    def part_copy(k):
        s = lax.rem(k, 2)
        return remote(part_out.at[s], part_in.at[s], part_send.at[s], part_recv.at[s], partner)

    def picked_copy(k):
        s = lax.rem(k, 2)
        return remote(
            picked.at[s], picked_in.at[s], picked_send.at[s], picked_recv.at[s], partner
        )

    def table_copy(o):
        return remote(
            tables.at[z], tables.at[z], table_send.at[o], table_recv.at[z], {"ep": 2 * o + core}
        )

    def load_fwd(k):
        s = lax.rem(k, 2)
        return pltpu.make_async_copy(weights.at[columns(k)], w_fwd.at[s], wf_sem.at[s])

    def load_bwd(k):
        s = lax.rem(k, 2)
        return pltpu.make_async_copy(weights.at[columns(k)], w_bwd.at[s], wb_sem.at[s])

    load_bwd(0).start()
    load_fwd(0).start()

    barrier = pltpu.get_barrier_semaphore()
    for device in (partner, after, before):
        pl.semaphore_signal(barrier, 1, device_id=device, device_id_type=pl.DeviceIdType.MESH)
    for o in range(chips):
        @pl.when(o != z)
        def _():
            pl.semaphore_signal(
                barrier, 1, device_id={"ep": 2 * o + core}, device_id_type=pl.DeviceIdType.MESH
            )

    experts = lax.broadcasted_iota(jnp.int32, (chips, tokens), 0)
    named = jnp.concatenate(
        [
            jnp.where(
                (routes[2 * i : 2 * i + 1, :] == experts)
                | (routes[2 * i + 1 : 2 * i + 2, :] == experts),
                1.0,
                0.0,
            )
            for i in range(2)
        ],
        axis=0,
    ).astype(F32)
    upto = jnp.where(
        lax.broadcasted_iota(jnp.int32, (tokens, tokens), 0)
        <= lax.broadcasted_iota(jnp.int32, (tokens, tokens), 1),
        1.0,
        0.0,
    ).astype(BF16)
    ordinal = dot(named.astype(BF16), upto, ((1,), (0,)))
    tables[z] = jnp.where(named > 0.5, ordinal - 1.0, -1.0)

    pl.semaphore_wait(barrier, 3 + last)
    for o in range(chips):
        @pl.when(o != z)
        def _():
            table_copy(o).start()
    lax.fori_loop(0, count, lambda k, c: (shift(k).start(), c)[1], 0)

    for parity, source in ((0, core), (1, other)):
        @pl.loop(0, chips)
        def _(o):
            gate = saved[o, source, :, :hid_units].astype(F32)
            up = saved[o, source, :, hid_units:].astype(F32)
            grad = upstream[o, source].astype(F32)
            sig = 1.0 / (1.0 + jnp.exp(-gate))
            grad_pre[parity, o, :, :hid_units] = (
                grad * up * sig * (1.0 + gate * (1.0 - sig))
            ).astype(BF16)
            grad_pre[parity, o, :, hid_units:] = (grad * gate * sig).astype(BF16)

    total[...] = jnp.zeros_like(total)

    for o in range(chips):
        @pl.when(o != z)
        def _():
            remote(
                tables.at[o], tables.at[o], table_send.at[o], table_recv.at[o], partner
            ).wait_recv()
    slots = lax.broadcasted_iota(jnp.int32, (capacity, tokens), 0).astype(F32)
    for o in range(chips):
        pick_fwd[o] = jnp.where(tables[o, pl.ds(z, 1), :] == slots, 1.0, 0.0).astype(BF16)
        pick_bwd[o] = jnp.where(tables[o, pl.ds(chips + z, 1), :] == slots, 1.0, 0.0).astype(BF16)

    def partial_rows(parity, s, target):
        @pl.loop(0, tiles)
        def _(i):
            grads = grad_pre[parity].reshape(chips * capacity, 2 * hid_units)
            product = dot(grads, w_bwd[s, tile(i), :], ((1,), (1,)))
            target[:, :, tile(i)] = product.astype(BF16).reshape(chips, capacity, TILE)

    def project(which, source, s):
        @pl.loop(0, 2 * hid_units // TILE)
        def _(i):
            data = source[...].reshape(chips * capacity, chunk)
            total[which, :, tile(i)] += dot(data, w_fwd[s, :, tile(i)], ((1,), (0,)))

    def add_landed(k, d):
        terms[k, d] = (terms[k, d].astype(F32) + landed[k, d].astype(F32)).astype(BF16)

    def step(t, carry):
        @pl.when(t < count)
        def _():
            s = lax.rem(t, 2)
            load_bwd(t).wait()

            @pl.when(t + 1 < count)
            def _():
                load_bwd(t + 1).start()

            @pl.when(t >= 2)
            def _():
                part_copy(t).wait_send()

            partial_rows(1, s, part_out.at[s])
            part_copy(t).start()
            shift(t).wait_recv()

            @pl.when(z < last)
            def _():
                row_up(t, z).start()

            @pl.when(z > 0)
            def _():
                row_down(t, z).start()

            partial_rows(0, s, part_own)
            part_copy(t).wait_recv()

            @pl.loop(0, chips)
            def _(o):
                @pl.loop(0, tiles)
                def _(i):
                    pair = (
                        part_own[o, :, tile(i)].astype(F32) + part_in[s, o, :, tile(i)].astype(F32)
                    ).astype(BF16)
                    terms[t, o, :, tile(i)] = dot(pick_bwd[o], pair, ((0,), (0,))).astype(BF16)

        up_k = t - z

        @pl.when((up_k >= 0) & (up_k < count) & (z < last))
        def _():
            for d in range(last, 0, -1):
                @pl.when(d > z)
                def _():
                    @pl.when(z > 0)
                    def _():
                        landing(up_k, d).wait_recv()
                        add_landed(up_k, d)

                    sum_up(up_k, d).start()

        down_k = t - (last - z)

        @pl.when((down_k >= 0) & (down_k < count) & (z > 0))
        def _():
            for d in range(last):
                @pl.when(d < z)
                def _():
                    @pl.when(z < last)
                    def _():
                        landing(down_k, d).wait_recv()
                        add_landed(down_k, d)

                    sum_down(down_k, d).start()

        for hop in range(1, chips):
            k = t - hop

            @pl.when((k >= 0) & (k < count))
            def _():
                @pl.when(z >= hop)
                def _():
                    o = jnp.maximum(z - hop, 0)
                    row_up(k, o).wait_recv()

                    @pl.when(z < last)
                    def _():
                        row_up(k, o).start()

                @pl.when(z + hop <= last)
                def _():
                    o = jnp.minimum(z + hop, last)
                    row_down(k, o).wait_recv()

                    @pl.when(z > 0)
                    def _():
                        row_down(k, o).start()

        end_k = t - last

        @pl.when((end_k >= 0) & (end_k < count))
        def _():
            result[end_k] = terms[end_k, z]

            @pl.when(z > 0)
            def _():
                landing(end_k, z).wait_recv()
                result[end_k] = (
                    result[end_k].astype(F32) + landed[end_k, z].astype(F32)
                ).astype(BF16)

            @pl.when(z < last)
            def _():
                landing(end_k, chips).wait_recv()
                result[end_k] = (
                    result[end_k].astype(F32) + landed[end_k, chips].astype(F32)
                ).astype(BF16)

            back(end_k).start()

        mul_k = t - chips

        @pl.when((mul_k >= 0) & (mul_k < count))
        def _():
            s = lax.rem(mul_k, 2)
            load_fwd(mul_k).wait()

            @pl.when(mul_k + 1 < count)
            def _():
                load_fwd(mul_k + 1).start()

            project(0, picked.at[s], s)
            picked_copy(mul_k).wait()
            project(1, picked_in.at[s], s)

        @pl.when((end_k >= 0) & (end_k < count))
        def _():
            s = lax.rem(end_k, 2)

            @pl.loop(0, chips)
            def _(o):
                @pl.loop(0, tiles)
                def _(i):
                    picked[s, o, :, tile(i)] = dot(
                        pick_fwd[o], rows[end_k, o, :, tile(i)], ((1,), (0,))
                    ).astype(BF16)

            picked_copy(end_k).start()

        return carry

    lax.fori_loop(0, count + chips, step, 0)

    for parity, source in ((0, core), (1, other)):
        @pl.loop(0, chips)
        def _(o):
            block = pl.ds(pl.multiple_of(o * capacity, capacity), capacity)
            gate = total[parity, block, :hid_units]
            up = total[parity, block, hid_units:]
            hidden[o, source] = (gate / (1.0 + jnp.exp(-gate)) * up).astype(BF16)

    def finish(k, carry):
        shift(k).wait_send()
        back(k).wait()
        for o in range(chips):
            @pl.when((o <= z) & (z < last))
            def _():
                row_up(k, o).wait_send()

            @pl.when((o >= z) & (z > 0))
            def _():
                row_down(k, o).wait_send()

            @pl.when(o != z)
            def _():
                sum_up(k, o).wait_send()

        return carry

    lax.fori_loop(0, count, finish, 0)
    for k in range(max(count - 2, 0), count):
        part_copy(k).wait_send()
    for o in range(chips):
        @pl.when(o != z)
        def _():
            table_copy(o).wait_send()


def kernel_form(prev_out, fwd_experts, expert_weights, bwd_experts, grad_hidden, saved_pre):
    groups, capacity, hid_units = grad_hidden.shape[2:]
    chips = groups // 2
    tokens, width = prev_out.shape[1:]
    chunk = CHUNK
    count = width // chunk
    routes = jnp.concatenate([fwd_experts[0], bwd_experts[0]], axis=1).T
    hbm = pl.BlockSpec(memory_space=pl.ANY)
    vmem = pl.BlockSpec(memory_space=pltpu.VMEM)
    dma = pltpu.SemaphoreType.DMA
    slots = chips * capacity
    hidden, grad_rows = pl.pallas_call(
        functools.partial(relay_kernel, chunk),
        out_shape=(
            jax.ShapeDtypeStruct((chips, 2, capacity, hid_units), BF16),
            jax.ShapeDtypeStruct((tokens, width), BF16),
        ),
        in_specs=[vmem, hbm, hbm, vmem, vmem],
        out_specs=(vmem, hbm),
        scratch_shapes=[
            pltpu.VMEM((count, chips, tokens, chunk), BF16),
            pltpu.VMEM((count, chips, tokens, chunk), BF16),
            pltpu.VMEM((count, chips + 1, tokens, chunk), BF16),
            pltpu.VMEM((2, chips, capacity, chunk), BF16),
            pltpu.VMEM((2, chips, capacity, chunk), BF16),
            pltpu.VMEM((2, chips, capacity, chunk), BF16),
            pltpu.VMEM((chips, capacity, chunk), BF16),
            pltpu.VMEM((2, chips, capacity, chunk), BF16),
            pltpu.VMEM((count, tokens, chunk), BF16),
            pltpu.VMEM((2, slots, 2 * hid_units), F32),
            pltpu.VMEM((2, chips, capacity, 2 * hid_units), BF16),
            pltpu.VMEM((2, chunk, 2 * hid_units), BF16),
            pltpu.VMEM((2, chunk, 2 * hid_units), BF16),
            pltpu.VMEM((chips, 2 * chips, tokens), F32),
            pltpu.VMEM((chips, capacity, tokens), BF16),
            pltpu.VMEM((chips, capacity, tokens), BF16),
            dma((count,)),
            dma((count, chips)),
            dma((count, chips + 1)),
            dma((count, chips + 1)),
            dma((count, chips)),
            dma((count,)),
            dma((count,)),
            dma((2,)),
            dma((2,)),
            dma((2,)),
            dma((2,)),
            dma((2,)),
            dma((2,)),
            dma((chips,)),
            dma((chips,)),
        ],
        compiler_params=pltpu.CompilerParams(
            collective_id=0, has_side_effects=True, vmem_limit_bytes=60 * 2**20
        ),
        cost_estimate=pl.CostEstimate(
            flops=8 * groups * capacity * width * hid_units,
            bytes_accessed=4 * width * hid_units,
            transcendentals=2 * groups * capacity * hid_units,
        ),
        name="relay",
    )(
        routes,
        prev_out[0],
        expert_weights[0, 0],
        grad_hidden.reshape(chips, 2, capacity, hid_units),
        saved_pre.reshape(chips, 2, capacity, 2 * hid_units),
    )
    return hidden.reshape(grad_hidden.shape), grad_rows[None]


def shards(prev_out, *rest):
    chips = lax.axis_size("ep") // 2
    held = 3 * chips * prev_out.shape[1] * prev_out.shape[2] * 2
    form = kernel_form if held <= RESIDENT and prev_out.shape[2] % CHUNK == 0 else permute_form
    return form(prev_out, *rest)


def solution(mesh):
    placed = (
        P("pp", "ep", None),
        P("pp", "ep", None),
        P("pp", "ep", None, None),
        P("pp", "ep", None),
        P("pp", "ep", None, None, None),
        P("pp", "ep", None, None, None),
    )
    return jax.shard_map(
        shards,
        mesh=mesh,
        in_specs=placed,
        out_specs=(P("pp", "ep", None, None, None), P("pp", "ep", None)),
        check_vma=False,
    )
```

```python
import functools

import jax
import jax.numpy as jnp
from jax import lax
from jax.experimental import pallas as pl
from jax.experimental.pallas import tpu as pltpu
from jax.sharding import PartitionSpec as P

PARTS = 2
CHUNK = 512
EARLY = 2
TILE = 256
RESIDENT = 40 * 2**20
F32 = jnp.float32
BF16 = jnp.bfloat16


def shifted(block, axis, distance):
    devices = range(lax.axis_size(axis))
    route = [((i - distance) % len(devices), i) for i in devices]
    return lax.ppermute(block, axis, route)


def partner_of(value):
    pairs = [(i, i ^ 1) for i in range(lax.axis_size("ep"))]
    return lax.ppermute(value, "ep", pairs)


def step_along(value, first, last, way):
    pairs = [(2 * z + c, 2 * (z + way) + c) for z in range(first, last + 1) for c in range(2)]
    return lax.ppermute(value, "ep", pairs)


def slots_of(route_ids, expert, capacity):
    named = jnp.any(route_ids == expert, axis=2).astype(jnp.int32)
    slot = jnp.cumsum(named, axis=1) - 1
    place = jnp.where(named == 1, slot, -1)
    return (place[:, None, :] == jnp.arange(capacity, dtype=jnp.int32)[None, :, None]).astype(
        jnp.bfloat16
    )


def swiglu_backward(upstream, saved):
    hid_units = upstream.shape[-1]
    pre_float = saved.astype(jnp.float32)
    gate_pre = pre_float[..., :hid_units]
    up_pre = pre_float[..., hid_units:]
    sigmoid_gate = jax.nn.sigmoid(gate_pre)
    upstream_float = upstream.astype(jnp.float32)
    grad_gate = upstream_float * up_pre * sigmoid_gate * (1.0 + gate_pre * (1.0 - sigmoid_gate))
    grad_up = upstream_float * gate_pre * sigmoid_gate
    return jnp.concatenate([grad_gate, grad_up], axis=-1).astype(jnp.bfloat16)


def permute_form(prev_out, fwd_experts, expert_weights, bwd_experts, grad_hidden, saved_pre):
    groups = lax.axis_size("ep")
    chips = groups // 2
    capacity = grad_hidden.shape[3]
    hid_units = grad_hidden.shape[4]
    width = prev_out.shape[2]
    part = width // PARTS
    weights = expert_weights[0, 0]
    me = lax.axis_index("ep")
    z, core = me // 2, me % 2
    tokens, top = fwd_experts.shape[1:]

    routes = lax.all_gather(
        jnp.concatenate([fwd_experts[0], bwd_experts[0]], axis=1), "ep", axis=0
    )
    fwd_pick = slots_of(routes[..., :top], z, capacity)
    bwd_pick = slots_of(routes[..., top:], z, capacity)
    fwd_own = lax.dynamic_index_in_dim(
        fwd_pick.reshape(chips, 2, capacity, tokens), core, 1, keepdims=False
    )
    bwd_own = lax.dynamic_index_in_dim(
        bwd_pick.reshape(chips, 2, capacity, tokens), core, 1, keepdims=False
    )

    grad_pre = swiglu_backward(grad_hidden[0, 0], saved_pre[0, 0])
    by_core = grad_pre.reshape(chips, 2, capacity, 2 * hid_units)
    grad_own = lax.dynamic_index_in_dim(by_core, core, 1, keepdims=False)
    grad_other = lax.dynamic_index_in_dim(by_core, 1 - core, 1, keepdims=False)

    projected_own = 0.0
    projected_other = 0.0
    grad_rows = []
    for k in range(PARTS):
        columns = slice(k * part, (k + 1) * part)
        own_weights = weights[columns]

        rows = shifted(prev_out[0, :, columns], "pp", 1)
        below, above = [], []
        up = down = rows
        for hop in range(1, chips):
            up = step_along(up, hop - 1, chips - 2, 1)
            down = step_along(down, 1, chips - hop, -1)
            below.insert(0, up)
            above.append(down)
        line = jnp.stack(below + [rows] + above)
        line = lax.dynamic_slice_in_dim(line, chips - 1 - z, chips, 0)
        picked = jnp.einsum(
            "nct,ntd->ncd", fwd_own, line, preferred_element_type=jnp.float32
        ).astype(jnp.bfloat16)
        picked_other = partner_of(picked)
        projected_own += jnp.einsum(
            "ncd,dh->nch", picked, own_weights, preferred_element_type=jnp.float32
        )
        projected_other += jnp.einsum(
            "ncd,dh->nch", picked_other, own_weights, preferred_element_type=jnp.float32
        )

        partial_other = jnp.einsum(
            "nch,dh->ncd", grad_other, own_weights, preferred_element_type=jnp.float32
        ).astype(jnp.bfloat16)
        received = partner_of(partial_other)
        partial_own = jnp.einsum(
            "nch,dh->ncd", grad_own, own_weights, preferred_element_type=jnp.float32
        ).astype(jnp.bfloat16)
        pair = (partial_own.astype(jnp.float32) + received.astype(jnp.float32)).astype(
            jnp.bfloat16
        )
        terms = jnp.einsum(
            "nct,ncd->ntd", bwd_own, pair, preferred_element_type=jnp.float32
        ).astype(jnp.bfloat16)
        up = down = 0.0
        for hop in range(1, chips):
            above_term = lax.dynamic_index_in_dim(
                terms, jnp.minimum(z + chips - hop, chips - 1), 0, keepdims=False
            )
            below_term = lax.dynamic_index_in_dim(
                terms, jnp.maximum(z - chips + hop, 0), 0, keepdims=False
            )
            up = step_along((above_term + up).astype(jnp.bfloat16), 0, hop - 1, 1)
            down = step_along((below_term + down).astype(jnp.bfloat16), chips - hop, chips - 1, -1)
        mine = lax.dynamic_index_in_dim(terms, z, 0, keepdims=False)
        grad_in = (
            mine.astype(jnp.float32) + up.astype(jnp.float32) + down.astype(jnp.float32)
        ).astype(jnp.bfloat16)
        grad_rows.append(shifted(grad_in, "pp", -1))

    def activated(projected):
        return (jax.nn.silu(projected[..., :hid_units]) * projected[..., hid_units:]).astype(
            jnp.bfloat16
        )

    own, other = activated(projected_own), activated(projected_other)
    hidden = jnp.stack(
        [jnp.where(core == 0, own, other), jnp.where(core == 0, other, own)], axis=1
    ).reshape(groups, capacity, hid_units)
    return hidden[None, None], jnp.concatenate(grad_rows, axis=1)[None]


def dot(a, b, dims):
    return lax.dot_general(a, b, (dims, ((), ())), preferred_element_type=F32)


def relay_kernel(
    chunk, routes, prev_out, weights, upstream, saved, hidden, grad_rows,
    rows, terms, landed, picked, picked_in, part_out, part_own, part_in, result,
    total, grad_pre, w_fwd, w_bwd, tables, pick_fwd, pick_bwd,
    shift_send, rows_recv, rows_send, land_recv, land_send, back_send, back_recv,
    picked_send, picked_recv, part_send, part_recv, wf_sem, wb_sem, table_send, table_recv,
):
    chips, _, capacity, hid_units = upstream.shape
    tokens, width = prev_out.shape
    count = width // chunk
    tiles = chunk // TILE
    sections = lax.axis_size("pp")
    me, section = lax.axis_index("ep"), lax.axis_index("pp")
    z, core = me // 2, me % 2
    other = 1 - core
    partner = {"ep": 2 * z + other}
    above = {"ep": jnp.minimum(me + 2, 2 * chips - 1)}
    below = {"ep": jnp.maximum(me - 2, 0)}
    after = {"pp": lax.rem(section + 1, sections)}
    before = {"pp": lax.rem(section + sections - 1, sections)}
    last = chips - 1

    def remote(src, dst, send, recv, device):
        return pltpu.make_async_remote_copy(
            src_ref=src, dst_ref=dst, send_sem=send, recv_sem=recv,
            device_id=device, device_id_type=pl.DeviceIdType.MESH,
        )

    def columns(k):
        return pl.ds(pl.multiple_of(k * chunk, chunk), chunk)

    def tile(i):
        return pl.ds(pl.multiple_of(i * TILE, TILE), TILE)

    def shift(k):
        return remote(
            prev_out.at[:, columns(k)], rows.at[k, z], shift_send.at[k], rows_recv.at[k, z], after
        )

    def row_up(k, o):
        return remote(rows.at[k, o], rows.at[k, o], rows_send.at[k, o], rows_recv.at[k, o], above)

    def row_down(k, o):
        slot = jnp.where(o == z, chips, o)
        return remote(
            rows.at[k, o], rows.at[k, o], rows_send.at[k, slot], rows_recv.at[k, o], below
        )

    def sum_up(k, d):
        return remote(
            terms.at[k, d], landed.at[k, d], land_send.at[k, d], land_recv.at[k, d], above
        )

    def sum_down(k, d):
        slot = jnp.where(d == z - 1, chips, d)
        return remote(
            terms.at[k, d], landed.at[k, slot], land_send.at[k, d], land_recv.at[k, slot], below
        )

    def landing(k, slot):
        return remote(
            terms.at[k, 0], landed.at[k, slot], land_send.at[k, 0], land_recv.at[k, slot], partner
        )

    def back(k):
        return remote(
            result.at[k], grad_rows.at[:, columns(k)], back_send.at[k], back_recv.at[k], before
        )

    def part_copy(k):
        s = lax.rem(k, 2)
        return remote(part_out.at[s], part_in.at[s], part_send.at[s], part_recv.at[s], partner)

    def picked_copy(k):
        s = lax.rem(k, 2)
        return remote(
            picked.at[s], picked_in.at[s], picked_send.at[s], picked_recv.at[s], partner
        )

    def table_copy(o):
        return remote(
            tables.at[z], tables.at[z], table_send.at[o], table_recv.at[z], {"ep": 2 * o + core}
        )

    def load_fwd(k):
        s = lax.rem(k, 2)
        return pltpu.make_async_copy(weights.at[columns(k)], w_fwd.at[s], wf_sem.at[s])

    def load_bwd(k):
        s = lax.rem(k, 2)
        return pltpu.make_async_copy(weights.at[columns(k)], w_bwd.at[s], wb_sem.at[s])

    load_bwd(0).start()
    load_fwd(0).start()

    barrier = pltpu.get_barrier_semaphore()
    for device in (partner, after, before):
        pl.semaphore_signal(barrier, 1, device_id=device, device_id_type=pl.DeviceIdType.MESH)
    for o in range(chips):
        @pl.when(o != z)
        def _():
            pl.semaphore_signal(
                barrier, 1, device_id={"ep": 2 * o + core}, device_id_type=pl.DeviceIdType.MESH
            )

    experts = lax.broadcasted_iota(jnp.int32, (chips, tokens), 0)
    named = jnp.concatenate(
        [
            jnp.where(
                (routes[2 * i : 2 * i + 1, :] == experts)
                | (routes[2 * i + 1 : 2 * i + 2, :] == experts),
                1.0,
                0.0,
            )
            for i in range(2)
        ],
        axis=0,
    ).astype(F32)
    upto = jnp.where(
        lax.broadcasted_iota(jnp.int32, (tokens, tokens), 0)
        <= lax.broadcasted_iota(jnp.int32, (tokens, tokens), 1),
        1.0,
        0.0,
    ).astype(BF16)
    ordinal = dot(named.astype(BF16), upto, ((1,), (0,)))
    tables[z] = jnp.where(named > 0.5, ordinal - 1.0, -1.0)

    pl.semaphore_wait(barrier, 3 + last)
    for o in range(chips):
        @pl.when(o != z)
        def _():
            table_copy(o).start()
    lax.fori_loop(0, count, lambda k, c: (shift(k).start(), c)[1], 0)

    early = min(EARLY, count)

    def send_own(k):
        shift(k).wait_recv()

        @pl.when(z < last)
        def _():
            row_up(k, z).start()

        @pl.when(z > 0)
        def _():
            row_down(k, z).start()

    for parity, source in ((1, other), (0, core)):
        if 1 - parity < early:
            send_own(1 - parity)

        @pl.loop(0, chips)
        def _(o):
            gate = saved[o, source, :, :hid_units].astype(F32)
            up = saved[o, source, :, hid_units:].astype(F32)
            grad = upstream[o, source].astype(F32)
            sig = 1.0 / (1.0 + jnp.exp(-gate))
            grad_pre[parity, o, :, :hid_units] = (
                grad * up * sig * (1.0 + gate * (1.0 - sig))
            ).astype(BF16)
            grad_pre[parity, o, :, hid_units:] = (grad * gate * sig).astype(BF16)

    total[...] = jnp.zeros_like(total)

    for o in range(chips):
        @pl.when(o != z)
        def _():
            remote(
                tables.at[o], tables.at[o], table_send.at[o], table_recv.at[o], partner
            ).wait_recv()
    slots = lax.broadcasted_iota(jnp.int32, (capacity, tokens), 0).astype(F32)
    for o in range(chips):
        pick_fwd[o] = jnp.where(tables[o, pl.ds(z, 1), :] == slots, 1.0, 0.0).astype(BF16)
        pick_bwd[o] = jnp.where(tables[o, pl.ds(chips + z, 1), :] == slots, 1.0, 0.0).astype(BF16)

    def partial_rows(parity, s, target):
        @pl.loop(0, tiles)
        def _(i):
            grads = grad_pre[parity].reshape(chips * capacity, 2 * hid_units)
            product = dot(grads, w_bwd[s, tile(i), :], ((1,), (1,)))
            target[:, :, tile(i)] = product.astype(BF16).reshape(chips, capacity, TILE)

    def project(which, source, s):
        @pl.loop(0, 2 * hid_units // TILE)
        def _(i):
            data = source[...].reshape(chips * capacity, chunk)
            total[which, :, tile(i)] += dot(data, w_fwd[s, :, tile(i)], ((1,), (0,)))

    def add_landed(k, d):
        terms[k, d] = (terms[k, d].astype(F32) + landed[k, d].astype(F32)).astype(BF16)

    def hop_rows(t, hop):
        k = t - hop

        @pl.when((k >= 0) & (k < count))
        def _():
            @pl.when(z >= hop)
            def _():
                o = jnp.maximum(z - hop, 0)
                row_up(k, o).wait_recv()

                @pl.when(z < last)
                def _():
                    row_up(k, o).start()

            @pl.when(z + hop <= last)
            def _():
                o = jnp.minimum(z + hop, last)
                row_down(k, o).wait_recv()

                @pl.when(z > 0)
                def _():
                    row_down(k, o).start()

    def sum_on(k, d, first, copy):
        @pl.when((k >= 0) & (k < count))
        def _():
            @pl.when(jnp.logical_not(first))
            def _():
                landing(k, d).wait_recv()
                add_landed(k, d)

            copy(k, d).start()

    def step(t, carry):
        @pl.when(t < count)
        def _():
            s = lax.rem(t, 2)

            @pl.when(t >= early)
            def _():
                send_own(t)

            load_bwd(t).wait()

            @pl.when(t + 1 < count)
            def _():
                load_bwd(t + 1).start()

            @pl.when(t >= 2)
            def _():
                part_copy(t).wait_send()

            partial_rows(1, s, part_out.at[s])
            part_copy(t).start()
            partial_rows(0, s, part_own)

        hop_rows(t, 1)

        @pl.when(t < count)
        def _():
            s = lax.rem(t, 2)
            part_copy(t).wait_recv()

            @pl.loop(0, chips)
            def _(o):
                @pl.loop(0, tiles)
                def _(i):
                    pair = (
                        part_own[o, :, tile(i)].astype(F32) + part_in[s, o, :, tile(i)].astype(F32)
                    ).astype(BF16)
                    terms[t, o, :, tile(i)] = dot(pick_bwd[o], pair, ((0,), (0,))).astype(BF16)

        for hop in range(2, chips):
            hop_rows(t, hop)

        for d in range(last, 0, -1):
            @pl.when(d > z + 1)
            def _():
                sum_on(t - z, d, z == 0, sum_up)

        for d in range(last):
            @pl.when(d < z - 1)
            def _():
                sum_on(t - last + z, d, z == last, sum_down)

        @pl.when(z < last)
        def _():
            sum_on(t - last + 1, jnp.minimum(z + 1, last), z == 0, sum_up)

        @pl.when(z > 0)
        def _():
            sum_on(t - last + 1, jnp.maximum(z - 1, 0), z == last, sum_down)

        end_k = t - last

        @pl.when((end_k >= 0) & (end_k < count))
        def _():
            result[end_k] = terms[end_k, z]

            @pl.when(z > 0)
            def _():
                landing(end_k, z).wait_recv()
                result[end_k] = (
                    result[end_k].astype(F32) + landed[end_k, z].astype(F32)
                ).astype(BF16)

            @pl.when(z < last)
            def _():
                landing(end_k, chips).wait_recv()
                result[end_k] = (
                    result[end_k].astype(F32) + landed[end_k, chips].astype(F32)
                ).astype(BF16)

            back(end_k).start()

        mul_k = t - chips

        @pl.when((mul_k >= 0) & (mul_k < count))
        def _():
            s = lax.rem(mul_k, 2)
            load_fwd(mul_k).wait()

            @pl.when(mul_k + 1 < count)
            def _():
                load_fwd(mul_k + 1).start()

            project(0, picked.at[s], s)
            picked_copy(mul_k).wait()
            project(1, picked_in.at[s], s)

        @pl.when((end_k >= 0) & (end_k < count))
        def _():
            s = lax.rem(end_k, 2)

            @pl.loop(0, chips)
            def _(o):
                @pl.loop(0, tiles)
                def _(i):
                    picked[s, o, :, tile(i)] = dot(
                        pick_fwd[o], rows[end_k, o, :, tile(i)], ((1,), (0,))
                    ).astype(BF16)

            picked_copy(end_k).start()

        return carry

    lax.fori_loop(0, count + chips, step, 0)

    for parity, source in ((0, core), (1, other)):
        @pl.loop(0, chips)
        def _(o):
            block = pl.ds(pl.multiple_of(o * capacity, capacity), capacity)
            gate = total[parity, block, :hid_units]
            up = total[parity, block, hid_units:]
            hidden[o, source] = (gate / (1.0 + jnp.exp(-gate)) * up).astype(BF16)

    def finish(k, carry):
        shift(k).wait_send()
        back(k).wait()
        for o in range(chips):
            @pl.when((o <= z) & (z < last))
            def _():
                row_up(k, o).wait_send()

            @pl.when((o >= z) & (z > 0))
            def _():
                row_down(k, o).wait_send()

            @pl.when(o != z)
            def _():
                sum_up(k, o).wait_send()

        return carry

    lax.fori_loop(0, count, finish, 0)
    for k in range(max(count - 2, 0), count):
        part_copy(k).wait_send()
    for o in range(chips):
        @pl.when(o != z)
        def _():
            table_copy(o).wait_send()


def kernel_form(prev_out, fwd_experts, expert_weights, bwd_experts, grad_hidden, saved_pre):
    groups, capacity, hid_units = grad_hidden.shape[2:]
    chips = groups // 2
    tokens, width = prev_out.shape[1:]
    chunk = CHUNK
    count = width // chunk
    routes = jnp.concatenate([fwd_experts[0], bwd_experts[0]], axis=1).T
    hbm = pl.BlockSpec(memory_space=pl.ANY)
    vmem = pl.BlockSpec(memory_space=pltpu.VMEM)
    dma = pltpu.SemaphoreType.DMA
    slots = chips * capacity
    hidden, grad_rows = pl.pallas_call(
        functools.partial(relay_kernel, chunk),
        out_shape=(
            jax.ShapeDtypeStruct((chips, 2, capacity, hid_units), BF16),
            jax.ShapeDtypeStruct((tokens, width), BF16),
        ),
        in_specs=[vmem, hbm, hbm, vmem, vmem],
        out_specs=(vmem, hbm),
        scratch_shapes=[
            pltpu.VMEM((count, chips, tokens, chunk), BF16),
            pltpu.VMEM((count, chips, tokens, chunk), BF16),
            pltpu.VMEM((count, chips + 1, tokens, chunk), BF16),
            pltpu.VMEM((2, chips, capacity, chunk), BF16),
            pltpu.VMEM((2, chips, capacity, chunk), BF16),
            pltpu.VMEM((2, chips, capacity, chunk), BF16),
            pltpu.VMEM((chips, capacity, chunk), BF16),
            pltpu.VMEM((2, chips, capacity, chunk), BF16),
            pltpu.VMEM((count, tokens, chunk), BF16),
            pltpu.VMEM((2, slots, 2 * hid_units), F32),
            pltpu.VMEM((2, chips, capacity, 2 * hid_units), BF16),
            pltpu.VMEM((2, chunk, 2 * hid_units), BF16),
            pltpu.VMEM((2, chunk, 2 * hid_units), BF16),
            pltpu.VMEM((chips, 2 * chips, tokens), F32),
            pltpu.VMEM((chips, capacity, tokens), BF16),
            pltpu.VMEM((chips, capacity, tokens), BF16),
            dma((count,)),
            dma((count, chips)),
            dma((count, chips + 1)),
            dma((count, chips + 1)),
            dma((count, chips)),
            dma((count,)),
            dma((count,)),
            dma((2,)),
            dma((2,)),
            dma((2,)),
            dma((2,)),
            dma((2,)),
            dma((2,)),
            dma((chips,)),
            dma((chips,)),
        ],
        compiler_params=pltpu.CompilerParams(
            collective_id=0, has_side_effects=True, vmem_limit_bytes=60 * 2**20
        ),
        cost_estimate=pl.CostEstimate(
            flops=8 * groups * capacity * width * hid_units,
            bytes_accessed=4 * width * hid_units,
            transcendentals=2 * groups * capacity * hid_units,
        ),
        name="relay",
    )(
        routes,
        prev_out[0],
        expert_weights[0, 0],
        grad_hidden.reshape(chips, 2, capacity, hid_units),
        saved_pre.reshape(chips, 2, capacity, 2 * hid_units),
    )
    return hidden.reshape(grad_hidden.shape), grad_rows[None]


def shards(prev_out, *rest):
    chips = lax.axis_size("ep") // 2
    held = 3 * chips * prev_out.shape[1] * prev_out.shape[2] * 2
    form = kernel_form if held <= RESIDENT and prev_out.shape[2] % CHUNK == 0 else permute_form
    return form(prev_out, *rest)


def solution(mesh):
    placed = (
        P("pp", "ep", None),
        P("pp", "ep", None),
        P("pp", "ep", None, None),
        P("pp", "ep", None),
        P("pp", "ep", None, None, None),
        P("pp", "ep", None, None, None),
    )
    return jax.shard_map(
        shards,
        mesh=mesh,
        in_specs=placed,
        out_specs=(P("pp", "ep", None, None, None), P("pp", "ep", None)),
        check_vma=False,
    )
```

```python
import functools

import jax
import jax.numpy as jnp
from jax import lax
from jax.experimental import pallas as pl
from jax.experimental.pallas import tpu as pltpu
from jax.sharding import PartitionSpec as P

PARTS = 2
CHUNK = 256
TILE = 256
RESIDENT = 40 * 2**20
F32 = jnp.float32
BF16 = jnp.bfloat16


def shifted(block, axis, distance):
    devices = range(lax.axis_size(axis))
    route = [((i - distance) % len(devices), i) for i in devices]
    return lax.ppermute(block, axis, route)


def partner_of(value):
    pairs = [(i, i ^ 1) for i in range(lax.axis_size("ep"))]
    return lax.ppermute(value, "ep", pairs)


def step_along(value, first, last, way):
    pairs = [(2 * z + c, 2 * (z + way) + c) for z in range(first, last + 1) for c in range(2)]
    return lax.ppermute(value, "ep", pairs)


def slots_of(route_ids, expert, capacity):
    named = jnp.any(route_ids == expert, axis=2).astype(jnp.int32)
    slot = jnp.cumsum(named, axis=1) - 1
    place = jnp.where(named == 1, slot, -1)
    return (place[:, None, :] == jnp.arange(capacity, dtype=jnp.int32)[None, :, None]).astype(
        jnp.bfloat16
    )


def swiglu_backward(upstream, saved):
    hid_units = upstream.shape[-1]
    pre_float = saved.astype(jnp.float32)
    gate_pre = pre_float[..., :hid_units]
    up_pre = pre_float[..., hid_units:]
    sigmoid_gate = jax.nn.sigmoid(gate_pre)
    upstream_float = upstream.astype(jnp.float32)
    grad_gate = upstream_float * up_pre * sigmoid_gate * (1.0 + gate_pre * (1.0 - sigmoid_gate))
    grad_up = upstream_float * gate_pre * sigmoid_gate
    return jnp.concatenate([grad_gate, grad_up], axis=-1).astype(jnp.bfloat16)


def permute_form(prev_out, fwd_experts, expert_weights, bwd_experts, grad_hidden, saved_pre):
    groups = lax.axis_size("ep")
    chips = groups // 2
    capacity = grad_hidden.shape[3]
    hid_units = grad_hidden.shape[4]
    width = prev_out.shape[2]
    part = width // PARTS
    weights = expert_weights[0, 0]
    me = lax.axis_index("ep")
    z, core = me // 2, me % 2
    tokens, top = fwd_experts.shape[1:]

    routes = lax.all_gather(
        jnp.concatenate([fwd_experts[0], bwd_experts[0]], axis=1), "ep", axis=0
    )
    fwd_pick = slots_of(routes[..., :top], z, capacity)
    bwd_pick = slots_of(routes[..., top:], z, capacity)
    fwd_own = lax.dynamic_index_in_dim(
        fwd_pick.reshape(chips, 2, capacity, tokens), core, 1, keepdims=False
    )
    bwd_own = lax.dynamic_index_in_dim(
        bwd_pick.reshape(chips, 2, capacity, tokens), core, 1, keepdims=False
    )

    grad_pre = swiglu_backward(grad_hidden[0, 0], saved_pre[0, 0])
    by_core = grad_pre.reshape(chips, 2, capacity, 2 * hid_units)
    grad_own = lax.dynamic_index_in_dim(by_core, core, 1, keepdims=False)
    grad_other = lax.dynamic_index_in_dim(by_core, 1 - core, 1, keepdims=False)

    projected_own = 0.0
    projected_other = 0.0
    grad_rows = []
    for k in range(PARTS):
        columns = slice(k * part, (k + 1) * part)
        own_weights = weights[columns]

        rows = shifted(prev_out[0, :, columns], "pp", 1)
        below, above = [], []
        up = down = rows
        for hop in range(1, chips):
            up = step_along(up, hop - 1, chips - 2, 1)
            down = step_along(down, 1, chips - hop, -1)
            below.insert(0, up)
            above.append(down)
        line = jnp.stack(below + [rows] + above)
        line = lax.dynamic_slice_in_dim(line, chips - 1 - z, chips, 0)
        picked = jnp.einsum(
            "nct,ntd->ncd", fwd_own, line, preferred_element_type=jnp.float32
        ).astype(jnp.bfloat16)
        picked_other = partner_of(picked)
        projected_own += jnp.einsum(
            "ncd,dh->nch", picked, own_weights, preferred_element_type=jnp.float32
        )
        projected_other += jnp.einsum(
            "ncd,dh->nch", picked_other, own_weights, preferred_element_type=jnp.float32
        )

        partial_other = jnp.einsum(
            "nch,dh->ncd", grad_other, own_weights, preferred_element_type=jnp.float32
        ).astype(jnp.bfloat16)
        received = partner_of(partial_other)
        partial_own = jnp.einsum(
            "nch,dh->ncd", grad_own, own_weights, preferred_element_type=jnp.float32
        ).astype(jnp.bfloat16)
        pair = (partial_own.astype(jnp.float32) + received.astype(jnp.float32)).astype(
            jnp.bfloat16
        )
        terms = jnp.einsum(
            "nct,ncd->ntd", bwd_own, pair, preferred_element_type=jnp.float32
        ).astype(jnp.bfloat16)
        up = down = 0.0
        for hop in range(1, chips):
            above_term = lax.dynamic_index_in_dim(
                terms, jnp.minimum(z + chips - hop, chips - 1), 0, keepdims=False
            )
            below_term = lax.dynamic_index_in_dim(
                terms, jnp.maximum(z - chips + hop, 0), 0, keepdims=False
            )
            up = step_along((above_term + up).astype(jnp.bfloat16), 0, hop - 1, 1)
            down = step_along((below_term + down).astype(jnp.bfloat16), chips - hop, chips - 1, -1)
        mine = lax.dynamic_index_in_dim(terms, z, 0, keepdims=False)
        grad_in = (
            mine.astype(jnp.float32) + up.astype(jnp.float32) + down.astype(jnp.float32)
        ).astype(jnp.bfloat16)
        grad_rows.append(shifted(grad_in, "pp", -1))

    def activated(projected):
        return (jax.nn.silu(projected[..., :hid_units]) * projected[..., hid_units:]).astype(
            jnp.bfloat16
        )

    own, other = activated(projected_own), activated(projected_other)
    hidden = jnp.stack(
        [jnp.where(core == 0, own, other), jnp.where(core == 0, other, own)], axis=1
    ).reshape(groups, capacity, hid_units)
    return hidden[None, None], jnp.concatenate(grad_rows, axis=1)[None]


def dot(a, b, dims):
    return lax.dot_general(a, b, (dims, ((), ())), preferred_element_type=F32)


def relay_kernel(
    chunk, routes, prev_out, weights, upstream, saved, hidden, grad_rows,
    rows, terms, landed, picked, picked_in, part_out, part_own, part_in, result,
    total, grad_pre, w_fwd, w_bwd, tables, pick_fwd, pick_bwd,
    shift_send, rows_recv, rows_send, land_recv, land_send, back_send, back_recv,
    picked_send, picked_recv, part_send, part_recv, wf_sem, wb_sem, table_send, table_recv,
):
    chips, _, capacity, hid_units = upstream.shape
    tokens, width = prev_out.shape
    count = width // chunk
    tiles = chunk // TILE
    sections = lax.axis_size("pp")
    me, section = lax.axis_index("ep"), lax.axis_index("pp")
    z, core = me // 2, me % 2
    other = 1 - core
    partner = {"ep": 2 * z + other}
    above = {"ep": jnp.minimum(me + 2, 2 * chips - 1)}
    below = {"ep": jnp.maximum(me - 2, 0)}
    after = {"pp": lax.rem(section + 1, sections)}
    before = {"pp": lax.rem(section + sections - 1, sections)}
    last = chips - 1

    def remote(src, dst, send, recv, device):
        return pltpu.make_async_remote_copy(
            src_ref=src, dst_ref=dst, send_sem=send, recv_sem=recv,
            device_id=device, device_id_type=pl.DeviceIdType.MESH,
        )

    def columns(k):
        return pl.ds(pl.multiple_of(k * chunk, chunk), chunk)

    def tile(i):
        return pl.ds(pl.multiple_of(i * TILE, TILE), TILE)

    def shift(k):
        return remote(
            prev_out.at[:, columns(k)], rows.at[k, z], shift_send.at[k], rows_recv.at[k, z], after
        )

    def row_up(k, o):
        return remote(rows.at[k, o], rows.at[k, o], rows_send.at[k, o], rows_recv.at[k, o], above)

    def row_down(k, o):
        slot = jnp.where(o == z, chips, o)
        return remote(
            rows.at[k, o], rows.at[k, o], rows_send.at[k, slot], rows_recv.at[k, o], below
        )

    def sum_up(k, d):
        return remote(
            terms.at[k, d], landed.at[k, d], land_send.at[k, d], land_recv.at[k, d], above
        )

    def sum_down(k, d):
        slot = jnp.where(d == z - 1, chips, d)
        return remote(
            terms.at[k, d], landed.at[k, slot], land_send.at[k, d], land_recv.at[k, slot], below
        )

    def landing(k, slot):
        return remote(
            terms.at[k, 0], landed.at[k, slot], land_send.at[k, 0], land_recv.at[k, slot], partner
        )

    def back(k):
        return remote(
            result.at[k], grad_rows.at[:, columns(k)], back_send.at[k], back_recv.at[k], before
        )

    def part_copy(k):
        s = lax.rem(k, 2)
        return remote(part_out.at[s], part_in.at[s], part_send.at[s], part_recv.at[s], partner)

    def picked_copy(k):
        s = lax.rem(k, 2)
        return remote(
            picked.at[s], picked_in.at[s], picked_send.at[s], picked_recv.at[s], partner
        )

    def table_copy(o):
        return remote(
            tables.at[z], tables.at[z], table_send.at[o], table_recv.at[z], {"ep": 2 * o + core}
        )

    def load_fwd(k):
        s = lax.rem(k, 2)
        return pltpu.make_async_copy(weights.at[columns(k)], w_fwd.at[s], wf_sem.at[s])

    def load_bwd(k):
        s = lax.rem(k, 2)
        return pltpu.make_async_copy(weights.at[columns(k)], w_bwd.at[s], wb_sem.at[s])

    load_bwd(0).start()
    load_fwd(0).start()

    barrier = pltpu.get_barrier_semaphore()
    for device in (partner, after, before):
        pl.semaphore_signal(barrier, 1, device_id=device, device_id_type=pl.DeviceIdType.MESH)
    for o in range(chips):
        @pl.when(o != z)
        def _():
            pl.semaphore_signal(
                barrier, 1, device_id={"ep": 2 * o + core}, device_id_type=pl.DeviceIdType.MESH
            )

    experts = lax.broadcasted_iota(jnp.int32, (chips, tokens), 0)
    named = jnp.concatenate(
        [
            jnp.where(
                (routes[2 * i : 2 * i + 1, :] == experts)
                | (routes[2 * i + 1 : 2 * i + 2, :] == experts),
                1.0,
                0.0,
            )
            for i in range(2)
        ],
        axis=0,
    ).astype(F32)
    upto = jnp.where(
        lax.broadcasted_iota(jnp.int32, (tokens, tokens), 0)
        <= lax.broadcasted_iota(jnp.int32, (tokens, tokens), 1),
        1.0,
        0.0,
    ).astype(BF16)
    ordinal = dot(named.astype(BF16), upto, ((1,), (0,)))
    tables[z] = jnp.where(named > 0.5, ordinal - 1.0, -1.0)

    pl.semaphore_wait(barrier, 3 + last)
    for o in range(chips):
        @pl.when(o != z)
        def _():
            table_copy(o).start()
    lax.fori_loop(0, count, lambda k, c: (shift(k).start(), c)[1], 0)

    early = min(chips, count)

    def send_own(k):
        shift(k).wait_recv()

        @pl.when(z < last)
        def _():
            row_up(k, z).start()

        @pl.when(z > 0)
        def _():
            row_down(k, z).start()

    for parity, source in ((1, other), (0, core)):
        @pl.loop(0, chips)
        def _(o):
            if parity:
                @pl.when(o < early)
                def _():
                    send_own(o)

            gate = saved[o, source, :, :hid_units].astype(F32)
            up = saved[o, source, :, hid_units:].astype(F32)
            grad = upstream[o, source].astype(F32)
            sig = 1.0 / (1.0 + jnp.exp(-gate))
            grad_pre[parity, o, :, :hid_units] = (
                grad * up * sig * (1.0 + gate * (1.0 - sig))
            ).astype(BF16)
            grad_pre[parity, o, :, hid_units:] = (grad * gate * sig).astype(BF16)

    total[...] = jnp.zeros_like(total)

    for o in range(chips):
        @pl.when(o != z)
        def _():
            remote(
                tables.at[o], tables.at[o], table_send.at[o], table_recv.at[o], partner
            ).wait_recv()
    slots = lax.broadcasted_iota(jnp.int32, (capacity, tokens), 0).astype(F32)
    for o in range(chips):
        pick_fwd[o] = jnp.where(tables[o, pl.ds(z, 1), :] == slots, 1.0, 0.0).astype(BF16)
        pick_bwd[o] = jnp.where(tables[o, pl.ds(chips + z, 1), :] == slots, 1.0, 0.0).astype(BF16)

    def partial_rows(parity, s, target):
        @pl.loop(0, tiles)
        def _(i):
            grads = grad_pre[parity].reshape(chips * capacity, 2 * hid_units)
            product = dot(grads, w_bwd[s, tile(i), :], ((1,), (1,)))
            target[:, :, tile(i)] = product.astype(BF16).reshape(chips, capacity, TILE)

    def project(which, source, s):
        @pl.loop(0, 2 * hid_units // TILE)
        def _(i):
            data = source[...].reshape(chips * capacity, chunk)
            total[which, :, tile(i)] += dot(data, w_fwd[s, :, tile(i)], ((1,), (0,)))

    def add_landed(k, d):
        terms[k, d] = (terms[k, d].astype(F32) + landed[k, d].astype(F32)).astype(BF16)

    def hop_rows(t, hop):
        k = t - hop

        @pl.when((k >= 0) & (k < count))
        def _():
            @pl.when(z >= hop)
            def _():
                o = jnp.maximum(z - hop, 0)
                row_up(k, o).wait_recv()

                @pl.when(z < last)
                def _():
                    row_up(k, o).start()

            @pl.when(z + hop <= last)
            def _():
                o = jnp.minimum(z + hop, last)
                row_down(k, o).wait_recv()

                @pl.when(z > 0)
                def _():
                    row_down(k, o).start()

    def sum_on(k, d, first, copy):
        @pl.when((k >= 0) & (k < count))
        def _():
            @pl.when(jnp.logical_not(first))
            def _():
                landing(k, d).wait_recv()
                add_landed(k, d)

            copy(k, d).start()

    def step(t, carry):
        @pl.when(t < count)
        def _():
            s = lax.rem(t, 2)

            @pl.when(t >= early)
            def _():
                send_own(t)

            load_bwd(t).wait()

            @pl.when(t + 1 < count)
            def _():
                load_bwd(t + 1).start()

            @pl.when(t >= 2)
            def _():
                part_copy(t).wait_send()

            partial_rows(1, s, part_out.at[s])
            part_copy(t).start()
            partial_rows(0, s, part_own)

        hop_rows(t, 1)

        @pl.when(t < count)
        def _():
            s = lax.rem(t, 2)
            part_copy(t).wait_recv()

            @pl.loop(0, chips)
            def _(o):
                @pl.loop(0, tiles)
                def _(i):
                    pair = (
                        part_own[o, :, tile(i)].astype(F32) + part_in[s, o, :, tile(i)].astype(F32)
                    ).astype(BF16)
                    terms[t, o, :, tile(i)] = dot(pick_bwd[o], pair, ((0,), (0,))).astype(BF16)

        for hop in range(2, chips):
            hop_rows(t, hop)

        for d in range(last, 0, -1):
            @pl.when(d > z + 1)
            def _():
                sum_on(t - z, d, z == 0, sum_up)

        for d in range(last):
            @pl.when(d < z - 1)
            def _():
                sum_on(t - last + z, d, z == last, sum_down)

        @pl.when(z < last)
        def _():
            sum_on(t - last + 1, jnp.minimum(z + 1, last), z == 0, sum_up)

        @pl.when(z > 0)
        def _():
            sum_on(t - last + 1, jnp.maximum(z - 1, 0), z == last, sum_down)

        end_k = t - last

        @pl.when((end_k >= 0) & (end_k < count))
        def _():
            result[end_k] = terms[end_k, z]

            @pl.when(z > 0)
            def _():
                landing(end_k, z).wait_recv()
                result[end_k] = (
                    result[end_k].astype(F32) + landed[end_k, z].astype(F32)
                ).astype(BF16)

            @pl.when(z < last)
            def _():
                landing(end_k, chips).wait_recv()
                result[end_k] = (
                    result[end_k].astype(F32) + landed[end_k, chips].astype(F32)
                ).astype(BF16)

            back(end_k).start()

        mul_k = t - chips

        @pl.when((mul_k >= 0) & (mul_k < count))
        def _():
            s = lax.rem(mul_k, 2)
            load_fwd(mul_k).wait()

            @pl.when(mul_k + 1 < count)
            def _():
                load_fwd(mul_k + 1).start()

            project(0, picked.at[s], s)
            picked_copy(mul_k).wait()
            project(1, picked_in.at[s], s)

        @pl.when((end_k >= 0) & (end_k < count))
        def _():
            s = lax.rem(end_k, 2)

            @pl.loop(0, chips)
            def _(o):
                @pl.loop(0, tiles)
                def _(i):
                    picked[s, o, :, tile(i)] = dot(
                        pick_fwd[o], rows[end_k, o, :, tile(i)], ((1,), (0,))
                    ).astype(BF16)

            picked_copy(end_k).start()

        return carry

    lax.fori_loop(0, count + chips, step, 0)

    for parity, source in ((0, core), (1, other)):
        @pl.loop(0, chips)
        def _(o):
            block = pl.ds(pl.multiple_of(o * capacity, capacity), capacity)
            gate = total[parity, block, :hid_units]
            up = total[parity, block, hid_units:]
            hidden[o, source] = (gate / (1.0 + jnp.exp(-gate)) * up).astype(BF16)

    def finish(k, carry):
        shift(k).wait_send()
        back(k).wait()
        for o in range(chips):
            @pl.when((o <= z) & (z < last))
            def _():
                row_up(k, o).wait_send()

            @pl.when((o >= z) & (z > 0))
            def _():
                row_down(k, o).wait_send()

            @pl.when(o != z)
            def _():
                sum_up(k, o).wait_send()

        return carry

    lax.fori_loop(0, count, finish, 0)
    for k in range(max(count - 2, 0), count):
        part_copy(k).wait_send()
    for o in range(chips):
        @pl.when(o != z)
        def _():
            table_copy(o).wait_send()


def kernel_form(prev_out, fwd_experts, expert_weights, bwd_experts, grad_hidden, saved_pre):
    groups, capacity, hid_units = grad_hidden.shape[2:]
    chips = groups // 2
    tokens, width = prev_out.shape[1:]
    chunk = CHUNK
    count = width // chunk
    routes = jnp.concatenate([fwd_experts[0], bwd_experts[0]], axis=1).T
    hbm = pl.BlockSpec(memory_space=pl.ANY)
    vmem = pl.BlockSpec(memory_space=pltpu.VMEM)
    dma = pltpu.SemaphoreType.DMA
    slots = chips * capacity
    hidden, grad_rows = pl.pallas_call(
        functools.partial(relay_kernel, chunk),
        out_shape=(
            jax.ShapeDtypeStruct((chips, 2, capacity, hid_units), BF16),
            jax.ShapeDtypeStruct((tokens, width), BF16),
        ),
        in_specs=[vmem, hbm, hbm, vmem, vmem],
        out_specs=(vmem, hbm),
        scratch_shapes=[
            pltpu.VMEM((count, chips, tokens, chunk), BF16),
            pltpu.VMEM((count, chips, tokens, chunk), BF16),
            pltpu.VMEM((count, chips + 1, tokens, chunk), BF16),
            pltpu.VMEM((2, chips, capacity, chunk), BF16),
            pltpu.VMEM((2, chips, capacity, chunk), BF16),
            pltpu.VMEM((2, chips, capacity, chunk), BF16),
            pltpu.VMEM((chips, capacity, chunk), BF16),
            pltpu.VMEM((2, chips, capacity, chunk), BF16),
            pltpu.VMEM((count, tokens, chunk), BF16),
            pltpu.VMEM((2, slots, 2 * hid_units), F32),
            pltpu.VMEM((2, chips, capacity, 2 * hid_units), BF16),
            pltpu.VMEM((2, chunk, 2 * hid_units), BF16),
            pltpu.VMEM((2, chunk, 2 * hid_units), BF16),
            pltpu.VMEM((chips, 2 * chips, tokens), F32),
            pltpu.VMEM((chips, capacity, tokens), BF16),
            pltpu.VMEM((chips, capacity, tokens), BF16),
            dma((count,)),
            dma((count, chips)),
            dma((count, chips + 1)),
            dma((count, chips + 1)),
            dma((count, chips)),
            dma((count,)),
            dma((count,)),
            dma((2,)),
            dma((2,)),
            dma((2,)),
            dma((2,)),
            dma((2,)),
            dma((2,)),
            dma((chips,)),
            dma((chips,)),
        ],
        compiler_params=pltpu.CompilerParams(
            collective_id=0, has_side_effects=True, vmem_limit_bytes=60 * 2**20
        ),
        cost_estimate=pl.CostEstimate(
            flops=8 * groups * capacity * width * hid_units,
            bytes_accessed=4 * width * hid_units,
            transcendentals=2 * groups * capacity * hid_units,
        ),
        name="relay",
    )(
        routes,
        prev_out[0],
        expert_weights[0, 0],
        grad_hidden.reshape(chips, 2, capacity, hid_units),
        saved_pre.reshape(chips, 2, capacity, 2 * hid_units),
    )
    return hidden.reshape(grad_hidden.shape), grad_rows[None]


def shards(prev_out, *rest):
    chips = lax.axis_size("ep") // 2
    held = 3 * chips * prev_out.shape[1] * prev_out.shape[2] * 2
    form = kernel_form if held <= RESIDENT and prev_out.shape[2] % CHUNK == 0 else permute_form
    return form(prev_out, *rest)


def solution(mesh):
    placed = (
        P("pp", "ep", None),
        P("pp", "ep", None),
        P("pp", "ep", None, None),
        P("pp", "ep", None),
        P("pp", "ep", None, None, None),
        P("pp", "ep", None, None, None),
    )
    return jax.shard_map(
        shards,
        mesh=mesh,
        in_specs=placed,
        out_specs=(P("pp", "ep", None, None, None), P("pp", "ep", None)),
        check_vma=False,
    )
```

```python
import functools

import jax
import jax.numpy as jnp
from jax import lax
from jax.experimental import pallas as pl
from jax.experimental.pallas import tpu as pltpu
from jax.sharding import PartitionSpec as P

PARTS = 2
CHUNK = 512
LEAD = 2
TILE = 256
RESIDENT = 40 * 2**20
F32 = jnp.float32
BF16 = jnp.bfloat16


def shifted(block, axis, distance):
    devices = range(lax.axis_size(axis))
    route = [((i - distance) % len(devices), i) for i in devices]
    return lax.ppermute(block, axis, route)


def partner_of(value):
    pairs = [(i, i ^ 1) for i in range(lax.axis_size("ep"))]
    return lax.ppermute(value, "ep", pairs)


def step_along(value, first, last, way):
    pairs = [(2 * z + c, 2 * (z + way) + c) for z in range(first, last + 1) for c in range(2)]
    return lax.ppermute(value, "ep", pairs)


def slots_of(route_ids, expert, capacity):
    named = jnp.any(route_ids == expert, axis=2).astype(jnp.int32)
    slot = jnp.cumsum(named, axis=1) - 1
    place = jnp.where(named == 1, slot, -1)
    return (place[:, None, :] == jnp.arange(capacity, dtype=jnp.int32)[None, :, None]).astype(
        jnp.bfloat16
    )


def swiglu_backward(upstream, saved):
    hid_units = upstream.shape[-1]
    pre_float = saved.astype(jnp.float32)
    gate_pre = pre_float[..., :hid_units]
    up_pre = pre_float[..., hid_units:]
    sigmoid_gate = jax.nn.sigmoid(gate_pre)
    upstream_float = upstream.astype(jnp.float32)
    grad_gate = upstream_float * up_pre * sigmoid_gate * (1.0 + gate_pre * (1.0 - sigmoid_gate))
    grad_up = upstream_float * gate_pre * sigmoid_gate
    return jnp.concatenate([grad_gate, grad_up], axis=-1).astype(jnp.bfloat16)


def permute_form(prev_out, fwd_experts, expert_weights, bwd_experts, grad_hidden, saved_pre):
    groups = lax.axis_size("ep")
    chips = groups // 2
    capacity = grad_hidden.shape[3]
    hid_units = grad_hidden.shape[4]
    width = prev_out.shape[2]
    part = width // PARTS
    weights = expert_weights[0, 0]
    me = lax.axis_index("ep")
    z, core = me // 2, me % 2
    tokens, top = fwd_experts.shape[1:]

    routes = lax.all_gather(
        jnp.concatenate([fwd_experts[0], bwd_experts[0]], axis=1), "ep", axis=0
    )
    fwd_pick = slots_of(routes[..., :top], z, capacity)
    bwd_pick = slots_of(routes[..., top:], z, capacity)
    fwd_own = lax.dynamic_index_in_dim(
        fwd_pick.reshape(chips, 2, capacity, tokens), core, 1, keepdims=False
    )
    bwd_own = lax.dynamic_index_in_dim(
        bwd_pick.reshape(chips, 2, capacity, tokens), core, 1, keepdims=False
    )

    grad_pre = swiglu_backward(grad_hidden[0, 0], saved_pre[0, 0])
    by_core = grad_pre.reshape(chips, 2, capacity, 2 * hid_units)
    grad_own = lax.dynamic_index_in_dim(by_core, core, 1, keepdims=False)
    grad_other = lax.dynamic_index_in_dim(by_core, 1 - core, 1, keepdims=False)

    projected_own = 0.0
    projected_other = 0.0
    grad_rows = []
    for k in range(PARTS):
        columns = slice(k * part, (k + 1) * part)
        own_weights = weights[columns]

        rows = shifted(prev_out[0, :, columns], "pp", 1)
        below, above = [], []
        up = down = rows
        for hop in range(1, chips):
            up = step_along(up, hop - 1, chips - 2, 1)
            down = step_along(down, 1, chips - hop, -1)
            below.insert(0, up)
            above.append(down)
        line = jnp.stack(below + [rows] + above)
        line = lax.dynamic_slice_in_dim(line, chips - 1 - z, chips, 0)
        picked = jnp.einsum(
            "nct,ntd->ncd", fwd_own, line, preferred_element_type=jnp.float32
        ).astype(jnp.bfloat16)
        picked_other = partner_of(picked)
        projected_own += jnp.einsum(
            "ncd,dh->nch", picked, own_weights, preferred_element_type=jnp.float32
        )
        projected_other += jnp.einsum(
            "ncd,dh->nch", picked_other, own_weights, preferred_element_type=jnp.float32
        )

        partial_other = jnp.einsum(
            "nch,dh->ncd", grad_other, own_weights, preferred_element_type=jnp.float32
        ).astype(jnp.bfloat16)
        received = partner_of(partial_other)
        partial_own = jnp.einsum(
            "nch,dh->ncd", grad_own, own_weights, preferred_element_type=jnp.float32
        ).astype(jnp.bfloat16)
        pair = (partial_own.astype(jnp.float32) + received.astype(jnp.float32)).astype(
            jnp.bfloat16
        )
        terms = jnp.einsum(
            "nct,ncd->ntd", bwd_own, pair, preferred_element_type=jnp.float32
        ).astype(jnp.bfloat16)
        up = down = 0.0
        for hop in range(1, chips):
            above_term = lax.dynamic_index_in_dim(
                terms, jnp.minimum(z + chips - hop, chips - 1), 0, keepdims=False
            )
            below_term = lax.dynamic_index_in_dim(
                terms, jnp.maximum(z - chips + hop, 0), 0, keepdims=False
            )
            up = step_along((above_term + up).astype(jnp.bfloat16), 0, hop - 1, 1)
            down = step_along((below_term + down).astype(jnp.bfloat16), chips - hop, chips - 1, -1)
        mine = lax.dynamic_index_in_dim(terms, z, 0, keepdims=False)
        grad_in = (
            mine.astype(jnp.float32) + up.astype(jnp.float32) + down.astype(jnp.float32)
        ).astype(jnp.bfloat16)
        grad_rows.append(shifted(grad_in, "pp", -1))

    def activated(projected):
        return (jax.nn.silu(projected[..., :hid_units]) * projected[..., hid_units:]).astype(
            jnp.bfloat16
        )

    own, other = activated(projected_own), activated(projected_other)
    hidden = jnp.stack(
        [jnp.where(core == 0, own, other), jnp.where(core == 0, other, own)], axis=1
    ).reshape(groups, capacity, hid_units)
    return hidden[None, None], jnp.concatenate(grad_rows, axis=1)[None]


def dot(a, b, dims):
    return lax.dot_general(a, b, (dims, ((), ())), preferred_element_type=F32)


def relay_kernel(
    chunk, routes, prev_out, weights, upstream, saved, hidden, grad_rows,
    rows, terms, landed, picked, picked_in, part_out, part_own, part_in, result,
    total, grad_pre, w_fwd, w_bwd, tables, pick_fwd, pick_bwd,
    shift_send, rows_recv, rows_send, land_recv, land_send, back_send, back_recv,
    picked_send, picked_recv, part_send, part_recv, wf_sem, wb_sem, table_send, table_recv,
):
    chips, _, capacity, hid_units = upstream.shape
    tokens, width = prev_out.shape
    count = width // chunk
    tiles = chunk // TILE
    sections = lax.axis_size("pp")
    me, section = lax.axis_index("ep"), lax.axis_index("pp")
    z, core = me // 2, me % 2
    other = 1 - core
    partner = {"ep": 2 * z + other}
    above = {"ep": jnp.minimum(me + 2, 2 * chips - 1)}
    below = {"ep": jnp.maximum(me - 2, 0)}
    after = {"pp": lax.rem(section + 1, sections)}
    before = {"pp": lax.rem(section + sections - 1, sections)}
    last = chips - 1

    def remote(src, dst, send, recv, device):
        return pltpu.make_async_remote_copy(
            src_ref=src, dst_ref=dst, send_sem=send, recv_sem=recv,
            device_id=device, device_id_type=pl.DeviceIdType.MESH,
        )

    def columns(k):
        return pl.ds(pl.multiple_of(k * chunk, chunk), chunk)

    def tile(i):
        return pl.ds(pl.multiple_of(i * TILE, TILE), TILE)

    def shift(k):
        return remote(
            prev_out.at[:, columns(k)], rows.at[k, z], shift_send.at[k], rows_recv.at[k, z], after
        )

    def row_up(k, o):
        return remote(rows.at[k, o], rows.at[k, o], rows_send.at[k, o], rows_recv.at[k, o], above)

    def row_down(k, o):
        slot = jnp.where(o == z, chips, o)
        return remote(
            rows.at[k, o], rows.at[k, o], rows_send.at[k, slot], rows_recv.at[k, o], below
        )

    def sum_up(k, d):
        return remote(
            terms.at[k, d], landed.at[k, d], land_send.at[k, d], land_recv.at[k, d], above
        )

    def sum_down(k, d):
        slot = jnp.where(d == z - 1, chips, d)
        return remote(
            terms.at[k, d], landed.at[k, slot], land_send.at[k, d], land_recv.at[k, slot], below
        )

    def landing(k, slot):
        return remote(
            terms.at[k, 0], landed.at[k, slot], land_send.at[k, 0], land_recv.at[k, slot], partner
        )

    def back(k):
        return remote(
            result.at[k], grad_rows.at[:, columns(k)], back_send.at[k], back_recv.at[k], before
        )

    def part_copy(k):
        s = lax.rem(k, 2)
        return remote(part_out.at[s], part_in.at[s], part_send.at[s], part_recv.at[s], partner)

    def picked_copy(k):
        s = lax.rem(k, 2)
        return remote(
            picked.at[s], picked_in.at[s], picked_send.at[s], picked_recv.at[s], partner
        )

    def table_copy(o):
        return remote(
            tables.at[z], tables.at[z], table_send.at[o], table_recv.at[z], {"ep": 2 * o + core}
        )

    def load_fwd(k):
        s = lax.rem(k, 2)
        return pltpu.make_async_copy(weights.at[columns(k)], w_fwd.at[s], wf_sem.at[s])

    def load_bwd(k):
        s = lax.rem(k, 2)
        return pltpu.make_async_copy(weights.at[columns(k)], w_bwd.at[s], wb_sem.at[s])

    load_bwd(0).start()
    load_fwd(0).start()

    barrier = pltpu.get_barrier_semaphore()
    for device in (partner, after, before):
        pl.semaphore_signal(barrier, 1, device_id=device, device_id_type=pl.DeviceIdType.MESH)
    for o in range(chips):
        @pl.when(o != z)
        def _():
            pl.semaphore_signal(
                barrier, 1, device_id={"ep": 2 * o + core}, device_id_type=pl.DeviceIdType.MESH
            )

    experts = lax.broadcasted_iota(jnp.int32, (chips, tokens), 0)
    named = jnp.concatenate(
        [
            jnp.where(
                (routes[2 * i : 2 * i + 1, :] == experts)
                | (routes[2 * i + 1 : 2 * i + 2, :] == experts),
                1.0,
                0.0,
            )
            for i in range(2)
        ],
        axis=0,
    ).astype(F32)
    upto = jnp.where(
        lax.broadcasted_iota(jnp.int32, (tokens, tokens), 0)
        <= lax.broadcasted_iota(jnp.int32, (tokens, tokens), 1),
        1.0,
        0.0,
    ).astype(BF16)
    ordinal = dot(named.astype(BF16), upto, ((1,), (0,)))
    tables[z] = jnp.where(named > 0.5, ordinal - 1.0, -1.0)

    pl.semaphore_wait(barrier, 3 + last)
    for o in range(chips):
        @pl.when(o != z)
        def _():
            table_copy(o).start()
    lax.fori_loop(0, count, lambda k, c: (shift(k).start(), c)[1], 0)

    early = min(chips, count)

    def send_own(k):
        shift(k).wait_recv()

        @pl.when(z < last)
        def _():
            row_up(k, z).start()

        @pl.when(z > 0)
        def _():
            row_down(k, z).start()

    for parity, source in ((1, other), (0, core)):
        @pl.loop(0, chips)
        def _(o):
            if parity:
                @pl.when(o < early)
                def _():
                    send_own(o)

            gate = saved[o, source, :, :hid_units].astype(F32)
            up = saved[o, source, :, hid_units:].astype(F32)
            grad = upstream[o, source].astype(F32)
            sig = 1.0 / (1.0 + jnp.exp(-gate))
            grad_pre[parity, o, :, :hid_units] = (
                grad * up * sig * (1.0 + gate * (1.0 - sig))
            ).astype(BF16)
            grad_pre[parity, o, :, hid_units:] = (grad * gate * sig).astype(BF16)

    total[...] = jnp.zeros_like(total)

    for o in range(chips):
        @pl.when(o != z)
        def _():
            remote(
                tables.at[o], tables.at[o], table_send.at[o], table_recv.at[o], partner
            ).wait_recv()
    slots = lax.broadcasted_iota(jnp.int32, (capacity, tokens), 0).astype(F32)
    for o in range(chips):
        pick_fwd[o] = jnp.where(tables[o, pl.ds(z, 1), :] == slots, 1.0, 0.0).astype(BF16)
        pick_bwd[o] = jnp.where(tables[o, pl.ds(chips + z, 1), :] == slots, 1.0, 0.0).astype(BF16)

    def partial_rows(parity, s, target):
        @pl.loop(0, tiles)
        def _(i):
            grads = grad_pre[parity].reshape(chips * capacity, 2 * hid_units)
            product = dot(grads, w_bwd[s, tile(i), :], ((1,), (1,)))
            target[:, :, tile(i)] = product.astype(BF16).reshape(chips, capacity, TILE)

    def project(which, source, s):
        @pl.loop(0, 2 * hid_units // TILE)
        def _(i):
            data = source[...].reshape(chips * capacity, chunk)
            total[which, :, tile(i)] += dot(data, w_fwd[s, :, tile(i)], ((1,), (0,)))

    def add_landed(k, d):
        terms[k, d] = (terms[k, d].astype(F32) + landed[k, d].astype(F32)).astype(BF16)

    def hop_rows(t, hop):
        k = t + LEAD - hop

        @pl.when((k >= 0) & (k < count))
        def _():
            @pl.when(z >= hop)
            def _():
                o = jnp.maximum(z - hop, 0)
                row_up(k, o).wait_recv()

                @pl.when(z < last)
                def _():
                    row_up(k, o).start()

            @pl.when(z + hop <= last)
            def _():
                o = jnp.minimum(z + hop, last)
                row_down(k, o).wait_recv()

                @pl.when(z > 0)
                def _():
                    row_down(k, o).start()

    def sum_on(k, d, first, copy):
        @pl.when((k >= 0) & (k < count))
        def _():
            @pl.when(jnp.logical_not(first))
            def _():
                landing(k, d).wait_recv()
                add_landed(k, d)

            copy(k, d).start()

    def step(t, carry):
        @pl.when((t + LEAD >= early) & (t + LEAD < count))
        def _():
            send_own(t + LEAD)

        @pl.when((t >= 0) & (t < count))
        def _():
            s = lax.rem(t, 2)
            load_bwd(t).wait()

            @pl.when(t + 1 < count)
            def _():
                load_bwd(t + 1).start()

            @pl.when(t >= 2)
            def _():
                part_copy(t).wait_send()

            partial_rows(1, s, part_out.at[s])
            part_copy(t).start()
            partial_rows(0, s, part_own)

        hop_rows(t, 1)

        @pl.when((t >= 0) & (t < count))
        def _():
            s = lax.rem(t, 2)
            part_copy(t).wait_recv()

            @pl.loop(0, chips)
            def _(o):
                @pl.loop(0, tiles)
                def _(i):
                    pair = (
                        part_own[o, :, tile(i)].astype(F32) + part_in[s, o, :, tile(i)].astype(F32)
                    ).astype(BF16)
                    terms[t, o, :, tile(i)] = dot(pick_bwd[o], pair, ((0,), (0,))).astype(BF16)

        for hop in range(2, chips):
            hop_rows(t, hop)

        for d in range(last, 0, -1):
            @pl.when(d > z + 1)
            def _():
                sum_on(t - z, d, z == 0, sum_up)

        for d in range(last):
            @pl.when(d < z - 1)
            def _():
                sum_on(t - last + z, d, z == last, sum_down)

        @pl.when(z < last)
        def _():
            sum_on(t - last + 1, jnp.minimum(z + 1, last), z == 0, sum_up)

        @pl.when(z > 0)
        def _():
            sum_on(t - last + 1, jnp.maximum(z - 1, 0), z == last, sum_down)

        end_k = t - last

        @pl.when((end_k >= 0) & (end_k < count))
        def _():
            result[end_k] = terms[end_k, z]

            @pl.when(z > 0)
            def _():
                landing(end_k, z).wait_recv()
                result[end_k] = (
                    result[end_k].astype(F32) + landed[end_k, z].astype(F32)
                ).astype(BF16)

            @pl.when(z < last)
            def _():
                landing(end_k, chips).wait_recv()
                result[end_k] = (
                    result[end_k].astype(F32) + landed[end_k, chips].astype(F32)
                ).astype(BF16)

            back(end_k).start()

        mul_k = t + LEAD - chips

        @pl.when((mul_k >= 0) & (mul_k < count))
        def _():
            s = lax.rem(mul_k, 2)
            load_fwd(mul_k).wait()

            @pl.when(mul_k + 1 < count)
            def _():
                load_fwd(mul_k + 1).start()

            project(0, picked.at[s], s)
            picked_copy(mul_k).wait()
            project(1, picked_in.at[s], s)

        pick_k = mul_k + 1

        @pl.when((pick_k >= 0) & (pick_k < count))
        def _():
            s = lax.rem(pick_k, 2)

            @pl.loop(0, chips)
            def _(o):
                @pl.loop(0, tiles)
                def _(i):
                    picked[s, o, :, tile(i)] = dot(
                        pick_fwd[o], rows[pick_k, o, :, tile(i)], ((1,), (0,))
                    ).astype(BF16)

            picked_copy(pick_k).start()

        return carry

    lax.fori_loop(-LEAD, count + chips, step, 0)

    for parity, source in ((0, core), (1, other)):
        @pl.loop(0, chips)
        def _(o):
            block = pl.ds(pl.multiple_of(o * capacity, capacity), capacity)
            gate = total[parity, block, :hid_units]
            up = total[parity, block, hid_units:]
            hidden[o, source] = (gate / (1.0 + jnp.exp(-gate)) * up).astype(BF16)

    def finish(k, carry):
        shift(k).wait_send()
        back(k).wait()
        for o in range(chips):
            @pl.when((o <= z) & (z < last))
            def _():
                row_up(k, o).wait_send()

            @pl.when((o >= z) & (z > 0))
            def _():
                row_down(k, o).wait_send()

            @pl.when(o != z)
            def _():
                sum_up(k, o).wait_send()

        return carry

    lax.fori_loop(0, count, finish, 0)
    for k in range(max(count - 2, 0), count):
        part_copy(k).wait_send()
    for o in range(chips):
        @pl.when(o != z)
        def _():
            table_copy(o).wait_send()


def kernel_form(prev_out, fwd_experts, expert_weights, bwd_experts, grad_hidden, saved_pre):
    groups, capacity, hid_units = grad_hidden.shape[2:]
    chips = groups // 2
    tokens, width = prev_out.shape[1:]
    chunk = CHUNK
    count = width // chunk
    routes = jnp.concatenate([fwd_experts[0], bwd_experts[0]], axis=1).T
    hbm = pl.BlockSpec(memory_space=pl.ANY)
    vmem = pl.BlockSpec(memory_space=pltpu.VMEM)
    dma = pltpu.SemaphoreType.DMA
    slots = chips * capacity
    hidden, grad_rows = pl.pallas_call(
        functools.partial(relay_kernel, chunk),
        out_shape=(
            jax.ShapeDtypeStruct((chips, 2, capacity, hid_units), BF16),
            jax.ShapeDtypeStruct((tokens, width), BF16),
        ),
        in_specs=[vmem, hbm, hbm, vmem, vmem],
        out_specs=(vmem, hbm),
        scratch_shapes=[
            pltpu.VMEM((count, chips, tokens, chunk), BF16),
            pltpu.VMEM((count, chips, tokens, chunk), BF16),
            pltpu.VMEM((count, chips + 1, tokens, chunk), BF16),
            pltpu.VMEM((2, chips, capacity, chunk), BF16),
            pltpu.VMEM((2, chips, capacity, chunk), BF16),
            pltpu.VMEM((2, chips, capacity, chunk), BF16),
            pltpu.VMEM((chips, capacity, chunk), BF16),
            pltpu.VMEM((2, chips, capacity, chunk), BF16),
            pltpu.VMEM((count, tokens, chunk), BF16),
            pltpu.VMEM((2, slots, 2 * hid_units), F32),
            pltpu.VMEM((2, chips, capacity, 2 * hid_units), BF16),
            pltpu.VMEM((2, chunk, 2 * hid_units), BF16),
            pltpu.VMEM((2, chunk, 2 * hid_units), BF16),
            pltpu.VMEM((chips, 2 * chips, tokens), F32),
            pltpu.VMEM((chips, capacity, tokens), BF16),
            pltpu.VMEM((chips, capacity, tokens), BF16),
            dma((count,)),
            dma((count, chips)),
            dma((count, chips + 1)),
            dma((count, chips + 1)),
            dma((count, chips)),
            dma((count,)),
            dma((count,)),
            dma((2,)),
            dma((2,)),
            dma((2,)),
            dma((2,)),
            dma((2,)),
            dma((2,)),
            dma((chips,)),
            dma((chips,)),
        ],
        compiler_params=pltpu.CompilerParams(
            collective_id=0, has_side_effects=True, vmem_limit_bytes=60 * 2**20
        ),
        cost_estimate=pl.CostEstimate(
            flops=8 * groups * capacity * width * hid_units,
            bytes_accessed=4 * width * hid_units,
            transcendentals=2 * groups * capacity * hid_units,
        ),
        name="relay",
    )(
        routes,
        prev_out[0],
        expert_weights[0, 0],
        grad_hidden.reshape(chips, 2, capacity, hid_units),
        saved_pre.reshape(chips, 2, capacity, 2 * hid_units),
    )
    return hidden.reshape(grad_hidden.shape), grad_rows[None]


def shards(prev_out, *rest):
    chips = lax.axis_size("ep") // 2
    held = 3 * chips * prev_out.shape[1] * prev_out.shape[2] * 2
    form = kernel_form if held <= RESIDENT and prev_out.shape[2] % CHUNK == 0 else permute_form
    return form(prev_out, *rest)


def solution(mesh):
    placed = (
        P("pp", "ep", None),
        P("pp", "ep", None),
        P("pp", "ep", None, None),
        P("pp", "ep", None),
        P("pp", "ep", None, None, None),
        P("pp", "ep", None, None, None),
    )
    return jax.shard_map(
        shards,
        mesh=mesh,
        in_specs=placed,
        out_specs=(P("pp", "ep", None, None, None), P("pp", "ep", None)),
        check_vma=False,
    )
```

```python
import functools

import jax
import jax.numpy as jnp
from jax import lax
from jax.experimental import pallas as pl
from jax.experimental.pallas import tpu as pltpu
from jax.sharding import PartitionSpec as P

PARTS = 2
CHUNK = 512
LEAD = 2
TILE = 256
RESIDENT = 40 * 2**20
F32 = jnp.float32
BF16 = jnp.bfloat16


def shifted(block, axis, distance):
    devices = range(lax.axis_size(axis))
    route = [((i - distance) % len(devices), i) for i in devices]
    return lax.ppermute(block, axis, route)


def partner_of(value):
    pairs = [(i, i ^ 1) for i in range(lax.axis_size("ep"))]
    return lax.ppermute(value, "ep", pairs)


def step_along(value, first, last, way):
    pairs = [(2 * z + c, 2 * (z + way) + c) for z in range(first, last + 1) for c in range(2)]
    return lax.ppermute(value, "ep", pairs)


def slots_of(route_ids, expert, capacity):
    named = jnp.any(route_ids == expert, axis=2).astype(jnp.int32)
    slot = jnp.cumsum(named, axis=1) - 1
    place = jnp.where(named == 1, slot, -1)
    return (place[:, None, :] == jnp.arange(capacity, dtype=jnp.int32)[None, :, None]).astype(
        jnp.bfloat16
    )


def swiglu_backward(upstream, saved):
    hid_units = upstream.shape[-1]
    pre_float = saved.astype(jnp.float32)
    gate_pre = pre_float[..., :hid_units]
    up_pre = pre_float[..., hid_units:]
    sigmoid_gate = jax.nn.sigmoid(gate_pre)
    upstream_float = upstream.astype(jnp.float32)
    grad_gate = upstream_float * up_pre * sigmoid_gate * (1.0 + gate_pre * (1.0 - sigmoid_gate))
    grad_up = upstream_float * gate_pre * sigmoid_gate
    return jnp.concatenate([grad_gate, grad_up], axis=-1).astype(jnp.bfloat16)


def permute_form(prev_out, fwd_experts, expert_weights, bwd_experts, grad_hidden, saved_pre):
    groups = lax.axis_size("ep")
    chips = groups // 2
    capacity = grad_hidden.shape[3]
    hid_units = grad_hidden.shape[4]
    width = prev_out.shape[2]
    part = width // PARTS
    weights = expert_weights[0, 0]
    me = lax.axis_index("ep")
    z, core = me // 2, me % 2
    tokens, top = fwd_experts.shape[1:]

    routes = lax.all_gather(
        jnp.concatenate([fwd_experts[0], bwd_experts[0]], axis=1), "ep", axis=0
    )
    fwd_pick = slots_of(routes[..., :top], z, capacity)
    bwd_pick = slots_of(routes[..., top:], z, capacity)
    fwd_own = lax.dynamic_index_in_dim(
        fwd_pick.reshape(chips, 2, capacity, tokens), core, 1, keepdims=False
    )
    bwd_own = lax.dynamic_index_in_dim(
        bwd_pick.reshape(chips, 2, capacity, tokens), core, 1, keepdims=False
    )

    grad_pre = swiglu_backward(grad_hidden[0, 0], saved_pre[0, 0])
    by_core = grad_pre.reshape(chips, 2, capacity, 2 * hid_units)
    grad_own = lax.dynamic_index_in_dim(by_core, core, 1, keepdims=False)
    grad_other = lax.dynamic_index_in_dim(by_core, 1 - core, 1, keepdims=False)

    projected_own = 0.0
    projected_other = 0.0
    grad_rows = []
    for k in range(PARTS):
        columns = slice(k * part, (k + 1) * part)
        own_weights = weights[columns]

        rows = shifted(prev_out[0, :, columns], "pp", 1)
        below, above = [], []
        up = down = rows
        for hop in range(1, chips):
            up = step_along(up, hop - 1, chips - 2, 1)
            down = step_along(down, 1, chips - hop, -1)
            below.insert(0, up)
            above.append(down)
        line = jnp.stack(below + [rows] + above)
        line = lax.dynamic_slice_in_dim(line, chips - 1 - z, chips, 0)
        picked = jnp.einsum(
            "nct,ntd->ncd", fwd_own, line, preferred_element_type=jnp.float32
        ).astype(jnp.bfloat16)
        picked_other = partner_of(picked)
        projected_own += jnp.einsum(
            "ncd,dh->nch", picked, own_weights, preferred_element_type=jnp.float32
        )
        projected_other += jnp.einsum(
            "ncd,dh->nch", picked_other, own_weights, preferred_element_type=jnp.float32
        )

        partial_other = jnp.einsum(
            "nch,dh->ncd", grad_other, own_weights, preferred_element_type=jnp.float32
        ).astype(jnp.bfloat16)
        received = partner_of(partial_other)
        partial_own = jnp.einsum(
            "nch,dh->ncd", grad_own, own_weights, preferred_element_type=jnp.float32
        ).astype(jnp.bfloat16)
        pair = (partial_own.astype(jnp.float32) + received.astype(jnp.float32)).astype(
            jnp.bfloat16
        )
        terms = jnp.einsum(
            "nct,ncd->ntd", bwd_own, pair, preferred_element_type=jnp.float32
        ).astype(jnp.bfloat16)
        up = down = 0.0
        for hop in range(1, chips):
            above_term = lax.dynamic_index_in_dim(
                terms, jnp.minimum(z + chips - hop, chips - 1), 0, keepdims=False
            )
            below_term = lax.dynamic_index_in_dim(
                terms, jnp.maximum(z - chips + hop, 0), 0, keepdims=False
            )
            up = step_along((above_term + up).astype(jnp.bfloat16), 0, hop - 1, 1)
            down = step_along((below_term + down).astype(jnp.bfloat16), chips - hop, chips - 1, -1)
        mine = lax.dynamic_index_in_dim(terms, z, 0, keepdims=False)
        grad_in = (
            mine.astype(jnp.float32) + up.astype(jnp.float32) + down.astype(jnp.float32)
        ).astype(jnp.bfloat16)
        grad_rows.append(shifted(grad_in, "pp", -1))

    def activated(projected):
        return (jax.nn.silu(projected[..., :hid_units]) * projected[..., hid_units:]).astype(
            jnp.bfloat16
        )

    own, other = activated(projected_own), activated(projected_other)
    hidden = jnp.stack(
        [jnp.where(core == 0, own, other), jnp.where(core == 0, other, own)], axis=1
    ).reshape(groups, capacity, hid_units)
    return hidden[None, None], jnp.concatenate(grad_rows, axis=1)[None]


def dot(a, b, dims):
    return lax.dot_general(a, b, (dims, ((), ())), preferred_element_type=F32)


def relay_kernel(
    chunk, routes, prev_out, weights, upstream, saved, hidden, grad_rows,
    rows, terms, landed, picked, picked_in, part_out, part_own, part_in, result,
    total, grad_pre, w_fwd, w_bwd, tables, pick_fwd, pick_bwd,
    shift_send, rows_recv, rows_send, land_recv, land_send, back_send, back_recv,
    picked_send, picked_recv, part_send, part_recv, wf_sem, wb_sem, table_send, table_recv,
):
    chips, _, capacity, hid_units = upstream.shape
    tokens, width = prev_out.shape
    count = width // chunk
    tiles = chunk // TILE
    sections = lax.axis_size("pp")
    me, section = lax.axis_index("ep"), lax.axis_index("pp")
    z, core = me // 2, me % 2
    other = 1 - core
    partner = {"ep": 2 * z + other}
    above = {"ep": jnp.minimum(me + 2, 2 * chips - 1)}
    below = {"ep": jnp.maximum(me - 2, 0)}
    after = {"pp": lax.rem(section + 1, sections)}
    before = {"pp": lax.rem(section + sections - 1, sections)}
    last = chips - 1

    def remote(src, dst, send, recv, device):
        return pltpu.make_async_remote_copy(
            src_ref=src, dst_ref=dst, send_sem=send, recv_sem=recv,
            device_id=device, device_id_type=pl.DeviceIdType.MESH,
        )

    def columns(k):
        return pl.ds(pl.multiple_of(k * chunk, chunk), chunk)

    def tile(i):
        return pl.ds(pl.multiple_of(i * TILE, TILE), TILE)

    def shift(k):
        return remote(
            prev_out.at[:, columns(k)], rows.at[k, z], shift_send.at[k], rows_recv.at[k, z], after
        )

    def row_up(k, o):
        return remote(rows.at[k, o], rows.at[k, o], rows_send.at[k, o], rows_recv.at[k, o], above)

    def row_down(k, o):
        slot = jnp.where(o == z, chips, o)
        return remote(
            rows.at[k, o], rows.at[k, o], rows_send.at[k, slot], rows_recv.at[k, o], below
        )

    def sum_up(k, d):
        return remote(
            terms.at[k, d], landed.at[k, d], land_send.at[k, d], land_recv.at[k, d], above
        )

    def sum_down(k, d):
        slot = jnp.where(d == z - 1, chips, d)
        return remote(
            terms.at[k, d], landed.at[k, slot], land_send.at[k, d], land_recv.at[k, slot], below
        )

    def landing(k, slot):
        return remote(
            terms.at[k, 0], landed.at[k, slot], land_send.at[k, 0], land_recv.at[k, slot], partner
        )

    def back(k):
        return remote(
            result.at[k], grad_rows.at[:, columns(k)], back_send.at[k], back_recv.at[k], before
        )

    def part_copy(k):
        s = lax.rem(k, 2)
        return remote(part_out.at[s], part_in.at[s], part_send.at[s], part_recv.at[s], partner)

    def picked_copy(k):
        s = lax.rem(k, 2)
        return remote(
            picked.at[s], picked_in.at[s], picked_send.at[s], picked_recv.at[s], partner
        )

    def table_copy(o):
        return remote(
            tables.at[z], tables.at[z], table_send.at[o], table_recv.at[z], {"ep": 2 * o + core}
        )

    def load_fwd(k):
        s = lax.rem(k, 2)
        return pltpu.make_async_copy(weights.at[columns(k)], w_fwd.at[s], wf_sem.at[s])

    def load_bwd(k):
        s = lax.rem(k, 2)
        return pltpu.make_async_copy(weights.at[columns(k)], w_bwd.at[s], wb_sem.at[s])

    load_bwd(0).start()
    load_fwd(0).start()

    barrier = pltpu.get_barrier_semaphore()
    for device in (partner, after, before):
        pl.semaphore_signal(barrier, 1, device_id=device, device_id_type=pl.DeviceIdType.MESH)
    for o in range(chips):
        @pl.when(o != z)
        def _():
            pl.semaphore_signal(
                barrier, 1, device_id={"ep": 2 * o + core}, device_id_type=pl.DeviceIdType.MESH
            )

    experts = lax.broadcasted_iota(jnp.int32, (chips, tokens), 0)
    named = jnp.concatenate(
        [
            jnp.where(
                (routes[2 * i : 2 * i + 1, :] == experts)
                | (routes[2 * i + 1 : 2 * i + 2, :] == experts),
                1.0,
                0.0,
            )
            for i in range(2)
        ],
        axis=0,
    ).astype(F32)
    upto = jnp.where(
        lax.broadcasted_iota(jnp.int32, (tokens, tokens), 0)
        <= lax.broadcasted_iota(jnp.int32, (tokens, tokens), 1),
        1.0,
        0.0,
    ).astype(BF16)
    ordinal = dot(named.astype(BF16), upto, ((1,), (0,)))
    tables[z] = jnp.where(named > 0.5, ordinal - 1.0, -1.0)

    pl.semaphore_wait(barrier, 3 + last)
    for o in range(chips):
        @pl.when(o != z)
        def _():
            table_copy(o).start()
    early = min(chips, count)
    for k in range(early):
        shift(k).start()

    def send_own(k):
        shift(k).wait_recv()

        @pl.when(k + early < count)
        def _():
            shift(k + early).start()

        @pl.when(z < last)
        def _():
            row_up(k, z).start()

        @pl.when(z > 0)
        def _():
            row_down(k, z).start()

    for parity, source in ((1, other), (0, core)):
        @pl.loop(0, chips)
        def _(o):
            if parity:
                @pl.when(o < early)
                def _():
                    send_own(o)

            gate = saved[o, source, :, :hid_units].astype(F32)
            up = saved[o, source, :, hid_units:].astype(F32)
            grad = upstream[o, source].astype(F32)
            sig = 1.0 / (1.0 + jnp.exp(-gate))
            grad_pre[parity, o, :, :hid_units] = (
                grad * up * sig * (1.0 + gate * (1.0 - sig))
            ).astype(BF16)
            grad_pre[parity, o, :, hid_units:] = (grad * gate * sig).astype(BF16)

    total[...] = jnp.zeros_like(total)

    for o in range(chips):
        @pl.when(o != z)
        def _():
            remote(
                tables.at[o], tables.at[o], table_send.at[o], table_recv.at[o], partner
            ).wait_recv()
    slots = lax.broadcasted_iota(jnp.int32, (capacity, tokens), 0).astype(F32)
    for o in range(chips):
        pick_fwd[o] = jnp.where(tables[o, pl.ds(z, 1), :] == slots, 1.0, 0.0).astype(BF16)
        pick_bwd[o] = jnp.where(tables[o, pl.ds(chips + z, 1), :] == slots, 1.0, 0.0).astype(BF16)

    def partial_rows(parity, s, target):
        @pl.loop(0, tiles)
        def _(i):
            grads = grad_pre[parity].reshape(chips * capacity, 2 * hid_units)
            product = dot(grads, w_bwd[s, tile(i), :], ((1,), (1,)))
            target[:, :, tile(i)] = product.astype(BF16).reshape(chips, capacity, TILE)

    def project(which, source, s):
        @pl.loop(0, 2 * hid_units // TILE)
        def _(i):
            data = source[...].reshape(chips * capacity, chunk)
            total[which, :, tile(i)] += dot(data, w_fwd[s, :, tile(i)], ((1,), (0,)))

    def add_landed(k, d):
        terms[k, d] = (terms[k, d].astype(F32) + landed[k, d].astype(F32)).astype(BF16)

    def hop_rows(t, hop):
        k = t + LEAD - hop

        @pl.when((k >= 0) & (k < count))
        def _():
            @pl.when(z >= hop)
            def _():
                o = jnp.maximum(z - hop, 0)
                row_up(k, o).wait_recv()

                @pl.when(z < last)
                def _():
                    row_up(k, o).start()

            @pl.when(z + hop <= last)
            def _():
                o = jnp.minimum(z + hop, last)
                row_down(k, o).wait_recv()

                @pl.when(z > 0)
                def _():
                    row_down(k, o).start()

    def sum_on(k, d, first, copy):
        @pl.when((k >= 0) & (k < count))
        def _():
            @pl.when(jnp.logical_not(first))
            def _():
                landing(k, d).wait_recv()
                add_landed(k, d)

            copy(k, d).start()

    def step(t, carry):
        @pl.when((t + LEAD >= early) & (t + LEAD < count))
        def _():
            send_own(t + LEAD)

        @pl.when((t >= 0) & (t < count))
        def _():
            s = lax.rem(t, 2)
            load_bwd(t).wait()

            @pl.when(t + 1 < count)
            def _():
                load_bwd(t + 1).start()

            @pl.when(t >= 2)
            def _():
                part_copy(t).wait_send()

            partial_rows(1, s, part_out.at[s])
            part_copy(t).start()
            partial_rows(0, s, part_own)

        hop_rows(t, 1)

        @pl.when((t >= 0) & (t < count))
        def _():
            s = lax.rem(t, 2)
            part_copy(t).wait_recv()

            @pl.loop(0, chips)
            def _(o):
                @pl.loop(0, tiles)
                def _(i):
                    pair = (
                        part_own[o, :, tile(i)].astype(F32) + part_in[s, o, :, tile(i)].astype(F32)
                    ).astype(BF16)
                    terms[t, o, :, tile(i)] = dot(pick_bwd[o], pair, ((0,), (0,))).astype(BF16)

        for hop in range(2, chips):
            hop_rows(t, hop)

        for d in range(last, 0, -1):
            @pl.when(d > z + 1)
            def _():
                sum_on(t - z, d, z == 0, sum_up)

        for d in range(last):
            @pl.when(d < z - 1)
            def _():
                sum_on(t - last + z, d, z == last, sum_down)

        @pl.when(z < last)
        def _():
            sum_on(t - last + 1, jnp.minimum(z + 1, last), z == 0, sum_up)

        @pl.when(z > 0)
        def _():
            sum_on(t - last + 1, jnp.maximum(z - 1, 0), z == last, sum_down)

        end_k = t - last

        @pl.when((end_k >= 0) & (end_k < count))
        def _():
            result[end_k] = terms[end_k, z]

            @pl.when(z > 0)
            def _():
                landing(end_k, z).wait_recv()
                result[end_k] = (
                    result[end_k].astype(F32) + landed[end_k, z].astype(F32)
                ).astype(BF16)

            @pl.when(z < last)
            def _():
                landing(end_k, chips).wait_recv()
                result[end_k] = (
                    result[end_k].astype(F32) + landed[end_k, chips].astype(F32)
                ).astype(BF16)

            back(end_k).start()

        mul_k = t + LEAD - chips

        @pl.when((mul_k >= 0) & (mul_k < count))
        def _():
            s = lax.rem(mul_k, 2)
            load_fwd(mul_k).wait()

            @pl.when(mul_k + 1 < count)
            def _():
                load_fwd(mul_k + 1).start()

            project(0, picked.at[s], s)
            picked_copy(mul_k).wait()
            project(1, picked_in.at[s], s)

        pick_k = mul_k + 1

        @pl.when((pick_k >= 0) & (pick_k < count))
        def _():
            s = lax.rem(pick_k, 2)

            @pl.loop(0, chips)
            def _(o):
                @pl.loop(0, tiles)
                def _(i):
                    picked[s, o, :, tile(i)] = dot(
                        pick_fwd[o], rows[pick_k, o, :, tile(i)], ((1,), (0,))
                    ).astype(BF16)

            picked_copy(pick_k).start()

        return carry

    lax.fori_loop(-LEAD, count + chips, step, 0)

    for parity, source in ((0, core), (1, other)):
        @pl.loop(0, chips)
        def _(o):
            block = pl.ds(pl.multiple_of(o * capacity, capacity), capacity)
            gate = total[parity, block, :hid_units]
            up = total[parity, block, hid_units:]
            hidden[o, source] = (gate / (1.0 + jnp.exp(-gate)) * up).astype(BF16)

    def finish(k, carry):
        shift(k).wait_send()
        back(k).wait()
        for o in range(chips):
            @pl.when((o <= z) & (z < last))
            def _():
                row_up(k, o).wait_send()

            @pl.when((o >= z) & (z > 0))
            def _():
                row_down(k, o).wait_send()

            @pl.when(o != z)
            def _():
                sum_up(k, o).wait_send()

        return carry

    lax.fori_loop(0, count, finish, 0)
    for k in range(max(count - 2, 0), count):
        part_copy(k).wait_send()
    for o in range(chips):
        @pl.when(o != z)
        def _():
            table_copy(o).wait_send()


def kernel_form(prev_out, fwd_experts, expert_weights, bwd_experts, grad_hidden, saved_pre):
    groups, capacity, hid_units = grad_hidden.shape[2:]
    chips = groups // 2
    tokens, width = prev_out.shape[1:]
    chunk = CHUNK
    count = width // chunk
    routes = jnp.concatenate([fwd_experts[0], bwd_experts[0]], axis=1).T
    hbm = pl.BlockSpec(memory_space=pl.ANY)
    vmem = pl.BlockSpec(memory_space=pltpu.VMEM)
    dma = pltpu.SemaphoreType.DMA
    slots = chips * capacity
    hidden, grad_rows = pl.pallas_call(
        functools.partial(relay_kernel, chunk),
        out_shape=(
            jax.ShapeDtypeStruct((chips, 2, capacity, hid_units), BF16),
            jax.ShapeDtypeStruct((tokens, width), BF16),
        ),
        in_specs=[vmem, hbm, hbm, vmem, vmem],
        out_specs=(vmem, hbm),
        scratch_shapes=[
            pltpu.VMEM((count, chips, tokens, chunk), BF16),
            pltpu.VMEM((count, chips, tokens, chunk), BF16),
            pltpu.VMEM((count, chips + 1, tokens, chunk), BF16),
            pltpu.VMEM((2, chips, capacity, chunk), BF16),
            pltpu.VMEM((2, chips, capacity, chunk), BF16),
            pltpu.VMEM((2, chips, capacity, chunk), BF16),
            pltpu.VMEM((chips, capacity, chunk), BF16),
            pltpu.VMEM((2, chips, capacity, chunk), BF16),
            pltpu.VMEM((count, tokens, chunk), BF16),
            pltpu.VMEM((2, slots, 2 * hid_units), F32),
            pltpu.VMEM((2, chips, capacity, 2 * hid_units), BF16),
            pltpu.VMEM((2, chunk, 2 * hid_units), BF16),
            pltpu.VMEM((2, chunk, 2 * hid_units), BF16),
            pltpu.VMEM((chips, 2 * chips, tokens), F32),
            pltpu.VMEM((chips, capacity, tokens), BF16),
            pltpu.VMEM((chips, capacity, tokens), BF16),
            dma((count,)),
            dma((count, chips)),
            dma((count, chips + 1)),
            dma((count, chips + 1)),
            dma((count, chips)),
            dma((count,)),
            dma((count,)),
            dma((2,)),
            dma((2,)),
            dma((2,)),
            dma((2,)),
            dma((2,)),
            dma((2,)),
            dma((chips,)),
            dma((chips,)),
        ],
        compiler_params=pltpu.CompilerParams(
            collective_id=0, has_side_effects=True, vmem_limit_bytes=60 * 2**20
        ),
        cost_estimate=pl.CostEstimate(
            flops=8 * groups * capacity * width * hid_units,
            bytes_accessed=4 * width * hid_units,
            transcendentals=2 * groups * capacity * hid_units,
        ),
        name="relay",
    )(
        routes,
        prev_out[0],
        expert_weights[0, 0],
        grad_hidden.reshape(chips, 2, capacity, hid_units),
        saved_pre.reshape(chips, 2, capacity, 2 * hid_units),
    )
    return hidden.reshape(grad_hidden.shape), grad_rows[None]


def shards(prev_out, *rest):
    chips = lax.axis_size("ep") // 2
    held = 3 * chips * prev_out.shape[1] * prev_out.shape[2] * 2
    form = kernel_form if held <= RESIDENT and prev_out.shape[2] % CHUNK == 0 else permute_form
    return form(prev_out, *rest)


def solution(mesh):
    placed = (
        P("pp", "ep", None),
        P("pp", "ep", None),
        P("pp", "ep", None, None),
        P("pp", "ep", None),
        P("pp", "ep", None, None, None),
        P("pp", "ep", None, None, None),
    )
    return jax.shard_map(
        shards,
        mesh=mesh,
        in_specs=placed,
        out_specs=(P("pp", "ep", None, None, None), P("pp", "ep", None)),
        check_vma=False,
    )
```
